256 devices in a mesh: pair: 8 (over z), slab: 32 (over x, y, core).
Axes of the slice: x: 4, y: 4, z: 8, core: 2. Of those that a mesh axis runs over, the one named last changes fastest.
Arguments:
- amplitudes: float32 [2048, 98304], P('pair', 'slab'), may hold values from -6 to 6
- integrals: float32 [4096, 98304], P(None, ('slab', 'pair')), may hold values from -0.078125 to 0.078125
- driver: float32 [2048, 4096], P('pair', 'slab'), may hold values from -6 to 6
- block_sizes: int32 [8], replicated, may hold values from 1 to 12288, 61440 in all
- pair_first: int32 [2048], P('pair'), may hold values from 0 to 99
- pair_second: int32 [2048], P('pair'), may hold values from 0 to 99
- ab_first: int32 [4096], P('slab'), may hold values from 0 to 999
- ab_second: int32 [4096], P('slab'), may hold values from 0 to 999
- occ_energy: float32 [100], replicated, may hold values from -2 to -0.5
- virt_energy: float32 [1000], replicated, may hold values from 0.3 to 3
Outputs:
- new_amplitudes: float32 [2048, 4096], P('pair', 'slab')
The draws below stay inside these ranges and needn't reach their ends.
Inputs may be any that keep to these rules, and one draw needn't show every extreme that they name: `block_sizes`: the largest block holds exactly 12288 live pairs; the sizes sum to 61440.
All inputs are finite; a program needn't handle non-finite values.
Results may differ from the reference program's by a relative error of at most 0.00011.
Values sent between devices are 32-bit elements; how exact they have to be, the bound alone decides.
A program may use at most 128 MiB of HBM per device.

```python
import math
import jax
import jax.numpy as jnp
import numpy as np
from jax import lax

NIRR = 8
CAP = 12288
NOCC = 100
NVIR = 1000
PAIRS = 2048
AB = 4096
CD = 98304


def set_ends(drawn, stream_key, smallest, largest):
    place = [jax.random.randint(jax.random.fold_in(stream_key, axis), (), 0, length) for axis, length in enumerate(drawn.shape)]
    main_axis = drawn.shape.index(max(drawn.shape))
    beside = place[:main_axis] + [(place[main_axis] + 1) % drawn.shape[main_axis]] + place[main_axis + 1:]
    return drawn.at[tuple(place)].set(smallest).at[tuple(beside)].set(largest)


def strengthened(entries, own_key, source, target, shards_of, factor):
    owner, partner = [(jnp.arange(entries.shape[axis_at]) // (entries.shape[axis_at] // shards_of)).reshape([-1 if axis == axis_at else 1 for axis in range(entries.ndim)]) for axis_at in (source, target)]
    chosen = jax.random.permutation(own_key, shards_of)[partner]
    strong = (owner == chosen) | (owner == (partner + shards_of // 2) % shards_of)
    return jnp.where(strong, factor * entries, entries)


def levels(rng, shape, shards, least, largest):
    gain, own = 1.0, jax.random.fold_in(rng, 6)
    for dim, blocks in shards:
        draws = jnp.exp(jax.random.uniform(jax.random.fold_in(own, dim), (blocks,), jnp.float32, least / len(shards), largest / len(shards)))
        gain = gain * jnp.repeat(draws, shape[dim] // blocks).reshape([-1 if axis == dim else 1 for axis in range(len(shape))])
    return gain


def profile(count, total, bound, slope):
    loads = [(1 << 20) // math.isqrt(standing ** slope) + 1 for standing in range(2, count + 1)]
    spare, given = total - bound - (count - 1), [1] * (count - 1)
    while spare > 0:
        movable = [i for i in range(count - 1) if given[i] < bound]
        mass, budget = sum([loads[i] for i in movable]), spare
        for i in movable:
            addition = min(bound - given[i], max(1, budget * loads[i] // mass), spare)
            given[i] = given[i] + addition
            spare = spare - addition
    return np.array([bound] + given)


def ragged_sizes(own_key, number_of, total, bound, slope):
    if number_of == 2:
        one = jax.random.randint(own_key, (), max(1, total - bound), min(bound, total - 1) + 1)
        return jnp.stack([one, total - one])
    lengths = jnp.asarray(profile(number_of, total, bound, slope), jnp.int32)
    pairs = (number_of - 1) // 2
    giver, receiver = lengths[1:1 + 2 * pairs:2], lengths[2:2 + 2 * pairs:2]
    room = jnp.minimum(giver - 1, bound - receiver)
    passed = jax.random.randint(jax.random.fold_in(own_key, 1), (pairs,), 0, 1 << 20) % (room + 1)
    lengths = lengths.at[1:1 + 2 * pairs:2].set(giver - passed).at[2:2 + 2 * pairs:2].set(receiver + passed)
    return lengths[jax.random.permutation(jax.random.fold_in(own_key, 2), number_of)]


def bell_draw(rng, dims, width, most, cuts=(), held_as=jnp.bfloat16):
    factor_of = levels(rng, dims, cuts, -0.22, 0.18) if cuts else 1.0
    result = jax.random.normal(rng, dims, jnp.float32) * width * factor_of
    return jnp.minimum(jnp.maximum(result, -most), most).astype(held_as)


def noise_with(key, shape, scale, most, shards, heavy, kind=jnp.bfloat16):
    result = scale * jax.random.normal(key, shape, jnp.float32)
    if shards:
        result = result * levels(key, shape, shards, -0.22, 0.18)
    return jnp.clip(strengthened(result, jax.random.fold_in(key, 3), *heavy), -most, most).astype(kind)


def setup_inputs(seed: int = 0) -> dict:
    arg_keys = jax.random.split(jax.random.key(seed), 11)
    return {
        "amplitudes": noise_with(arg_keys[0], (PAIRS, CD), 1.0, 6.0, ((0, 8), (1, 32)), (1, 0, 32, 2.75), jnp.float32),
        "integrals": noise_with(arg_keys[1], (AB, CD), CD ** -0.5, 0.078125, ((1, 256),), (1, 0, 256, 6.0), jnp.float32),
        "driver": bell_draw(arg_keys[2], (PAIRS, AB), 1.0, 6.0, ((0, 8), (1, 32)), jnp.float32),
        "block_sizes": ragged_sizes(arg_keys[3], NIRR, 5 * CAP, CAP, 2).astype(jnp.int32),
        "pair_first": set_ends(jax.random.randint(arg_keys[4], (PAIRS,), 0, NOCC), jax.random.fold_in(arg_keys[4], 1), 0, NOCC - 1).astype(jnp.int32),
        "pair_second": set_ends(jax.random.randint(arg_keys[5], (PAIRS,), 0, NOCC), jax.random.fold_in(arg_keys[5], 1), 0, NOCC - 1).astype(jnp.int32),
        "ab_first": set_ends(jax.random.randint(arg_keys[6], (AB,), 0, NVIR), jax.random.fold_in(arg_keys[6], 1), 0, NVIR - 1).astype(jnp.int32),
        "ab_second": set_ends(jax.random.randint(arg_keys[7], (AB,), 0, NVIR), jax.random.fold_in(arg_keys[7], 1), 0, NVIR - 1).astype(jnp.int32),
        "occ_energy": jnp.clip(jax.random.uniform(arg_keys[8], (NOCC,), jnp.float32, -2.0, -0.5), -2.0, -0.5),
        "virt_energy": jnp.clip(jax.random.uniform(arg_keys[9], (NVIR,), jnp.float32, 0.3, 3.0), 0.3, 3.0),
    }


def reference(amplitudes, integrals, driver, block_sizes, pair_first, pair_second, ab_first, ab_second, occ_energy, virt_energy):
    column = jnp.arange(NIRR * CAP, dtype=jnp.int32)
    limit = block_sizes[(column // CAP).astype(jnp.int32)]
    live = (column % CAP) < limit
    masked = jnp.where(live[None, :], amplitudes, jnp.zeros((), amplitudes.dtype))
    ladder = lax.dot_general(masked, integrals, (((1,), (1,)), ((), ())), precision=lax.Precision.HIGHEST, preferred_element_type=jnp.float32)
    occupied = occ_energy[pair_first] + occ_energy[pair_second]
    denominator = occupied[:, None] - virt_energy[ab_first][None, :] - virt_energy[ab_second][None, :]
    return (driver + ladder) / denominator
```

```python
import functools

import jax
import jax.numpy as jnp
from jax import lax
from jax.experimental import pallas as pl
from jax.experimental.pallas import tpu as pltpu
from jax.sharding import PartitionSpec as P

MESH = pl.DeviceIdType.MESH
NT = (((1,), (1,)), ((), ()))

NZ = 8
NX = 4
ROWS = 256
KD = 384
COLS = 128
SUB = 64
PER = COLS // SUB
QUART = SUB // 2
STEPS = NZ * PER
LANES = 128
MROWS = 2 * NX * SUB
RING = 4
A_BEGIN = ((0, (3, 4)), (PER, (5, 6)))
LEG1_BEGIN = 2 * PER
LEG2_BEGIN = 9 * PER // 2
Z_BEGIN = 6 * PER
ORDER = (0, 1, 7, 2, 6, 3, 5, 4)


def split(v):
    hi = v.astype(jnp.bfloat16)
    lo = (v - hi.astype(jnp.float32)).astype(jnp.bfloat16)
    return hi, lo


def ladder_kernel(
    sizes, a_hbm, b_hbm, out,
    a_own, a_sib, relay, b_own, b_sib, a3, b3, part, quad, done,
    r1, r2, r3, r4, zr,
    loc_sem, bl, bs, br, as_, ar, hs, hr, fs, fr, s1, q1, s2, q2, s3, q3, s4, q4, zs, zq,
):
    z = lax.axis_index("pair")
    s = lax.axis_index("slab")
    x, y, c = s // (2 * NX), (s // 2) % NX, s % 2

    def slab(xx, yy, cc):
        return (xx * NX + yy) * 2 + cc

    def up(v, n, d):
        return lax.rem(v + d, n)

    xp, xo, xm = up(x, NX, 1), up(x, NX, 2), up(x, NX, 3)
    yp, yo, ym = up(y, NX, 1), up(y, NX, 2), up(y, NX, 3)
    sibling = (z, slab(x, y, 1 - c))
    side = ((z, slab(xp, y, c)), (z, slab(xm, y, c)), (z, slab(x, yp, c)), (z, slab(x, ym, c)))

    def zdev(d):
        return (up(z, NZ, d), s)

    def remote(src, dst, send, recv, dev):
        return pltpu.make_async_remote_copy(
            src_ref=src, dst_ref=dst, send_sem=send, recv_sem=recv, device_id=dev, device_id_type=MESH
        )

    barrier = pltpu.get_barrier_semaphore()
    peers = [sibling, *side] + [zdev(d) for d in range(1, NZ)]
    for dev in peers:
        pl.semaphore_signal(barrier, inc=1, device_id=dev, device_id_type=MESH)
    pl.semaphore_wait(barrier, len(peers))

    def acols(d):
        return pl.ds(pl.multiple_of(up(z, NZ, d) * KD, KD), KD)

    def b_load(h):
        return pltpu.make_async_copy(b_hbm.at[:, c, pl.ds(h * SUB, SUB)], b_own.at[h], bl.at[h])

    def b_swap(h):
        return remote(b_hbm.at[:, 1 - c, pl.ds(h * SUB, SUB)], b_sib.at[h], bs.at[h], br.at[h], sibling)

    a_loc = pltpu.make_async_copy(a_hbm.at[:, acols(0)], a_own.at[0], loc_sem)
    a_swap = remote(a_hbm.at[:, acols(0)], a_sib.at[0], fs.at[0], fr.at[0], sibling)
    b_swap(0).start()
    b_load(0).start()
    a_swap.start()
    a_loc.start()
    for h in range(1, PER):
        b_swap(h).start()
        b_load(h).start()

    def a_send(k):
        d = NZ - ORDER[k]
        return remote(a_hbm.at[:, acols(d)], a_own.at[k], as_.at[k], ar.at[k], zdev(d))

    def leg1(h):
        rows = pl.ds(h * (ROWS // 2), ROWS // 2)
        return remote(a_hbm.at[rows, acols(4)], relay.at[h], hs.at[h], hr.at[h], zdev((2, 6)[h]))

    def leg2(h):
        rows = pl.ds(h * (ROWS // 2), ROWS // 2)
        return remote(relay.at[h], a_own.at[NZ - 1, rows], hs.at[2 + h], hr.at[2 + h], zdev((2, 6)[h]))

    def forward(k):
        return remote(a_own.at[k], a_sib.at[k], fs.at[k], fr.at[k], sibling)

    for k in (1, 2):
        a_send(k).start()

    limit = sizes[s // 4]
    column = lax.broadcasted_iota(jnp.int32, (SUB, KD), 1)

    def convert(src, h, first, slab_at):
        live = column < limit - (slab_at % 4) * (NZ * KD) - z * KD

        def one(j, carry):
            hi, lo = split(jnp.where(live, src[h, j], 0.0))
            rows = pl.ds(pl.multiple_of(j * SUB, SUB), SUB)
            b3[h, rows, pl.ds(first, KD)] = hi
            b3[h, rows, pl.ds(2 * KD + first, KD)] = lo
            b3[h, rows, pl.ds(4 * KD + first, KD)] = hi
            return carry

        lax.fori_loop(0, NX * NX, one, 0)

    def send1(i):
        p = lax.rem(i, RING)
        src = (
            part.at[p, 0, xo, :, pl.ds(0, QUART)],
            part.at[p, 0, xo, :, pl.ds(QUART, QUART)],
            part.at[p, 1, :, yo, pl.ds(0, QUART)],
            part.at[p, 1, :, yo, pl.ds(QUART, QUART)],
        )
        return [remote(src[k], r1.at[p, k], s1.at[p, k], q1.at[p, k], side[k]) for k in range(4)]

    def send2(i):
        p = lax.rem(i, RING)
        src = (part.at[p, 0, xp], part.at[p, 0, xm], part.at[p, 1, :, yp], part.at[p, 1, :, ym])
        return [remote(src[k], r2.at[p, k], s2.at[p, k], q2.at[p, k], side[k]) for k in range(4)]

    def send3(i):
        p = lax.rem(i, RING)
        src = (
            quad.at[p, 1, xo, pl.ds(0, QUART)],
            quad.at[p, 1, xo, pl.ds(QUART, QUART)],
            quad.at[p, 0, yo, pl.ds(0, QUART)],
            quad.at[p, 0, yo, pl.ds(QUART, QUART)],
        )
        return [remote(src[k], r3.at[p, k], s3.at[p, k], q3.at[p, k], side[k]) for k in range(4)]

    def send4(i):
        p = lax.rem(i, RING)
        src = (quad.at[p, 1, xp], quad.at[p, 1, xm], quad.at[p, 0, yp], quad.at[p, 0, ym])
        return [remote(src[k], r4.at[p, k], s4.at[p, k], q4.at[p, k], side[k]) for k in range(4)]

    def zsend(i):
        k, h = i // PER, lax.rem(i, PER)
        d = jnp.where(lax.rem(k, 2) == 1, (k + 1) // 2, NZ - k // 2)
        return remote(done.at[i], zr.at[k, h], zs.at[i], zq.at[i], zdev(d))

    def stage1(i):
        p = lax.rem(i, RING)
        k = i // PER
        h = lax.rem(i, PER)

        for step_at in range(PER):
            @pl.when(i == step_at)
            def _():
                b_load(step_at).wait()
                convert(b_own, step_at, 0, s)
                if step_at == 0:
                    a_loc.wait()
                b_swap(step_at).wait()
                convert(b_sib, step_at, KD, slab(x, y, 1 - c))

        @pl.when(h == 0)
        def _():
            forward(k).wait_recv()
            for first, source in ((0, a_own), (KD, a_sib)):
                hi, lo = split(source[k])
                a3[:, pl.ds(first, KD)] = hi
                a3[:, pl.ds(2 * KD + first, KD)] = hi
                a3[:, pl.ds(4 * KD + first, KD)] = lo

        def columns(m, carry):
            rows = pl.ds(pl.multiple_of(m * MROWS, MROWS), MROWS)
            acc = lax.dot_general(b3[h, rows, :], a3[...], NT, preferred_element_type=jnp.float32)
            for xx in range(2):
                for yy in range(NX):
                    at = (xx * NX + yy) * SUB
                    for half in range(2):
                        part[p, half, 2 * m + xx, yy] = acc[at:at + SUB, half * LANES:(half + 1) * LANES]
            return carry

        lax.fori_loop(0, NX // 2, columns, 0)
        for copy in send1(i):
            copy.start()

        for begin, blocks in A_BEGIN:
            @pl.when(i == begin)
            def _():
                for kk in blocks:
                    a_send(kk).start()

        @pl.when(i == LEG1_BEGIN)
        def _():
            for half in range(2):
                leg1(half).start()

        @pl.when(i == LEG2_BEGIN)
        def _():
            for half in range(2):
                leg1(half).wait_recv()
                leg2(half).start()

    def fetch(i):
        k = i // PER

        @pl.when(k < NZ - 2)
        def _():
            a_wait = remote(a_own.at[k + 1], a_own.at[k + 1], as_.at[k + 1], ar.at[k + 1], sibling)
            a_wait.wait_recv()
            forward(k + 1).start()

        @pl.when(k == NZ - 2)
        def _():
            for half in range(2):
                leg2(half).wait_recv()
            forward(NZ - 1).start()

    def stage2(i):
        p = lax.rem(i, RING)
        for copy in send1(i):
            copy.wait()
        part[p, 0, xp, :, pl.ds(0, QUART)] += r1[p, 0]
        part[p, 0, xm, :, pl.ds(QUART, QUART)] += r1[p, 1]
        part[p, 1, :, yp, pl.ds(0, QUART)] += r1[p, 2]
        part[p, 1, :, ym, pl.ds(QUART, QUART)] += r1[p, 3]
        for copy in send2(i):
            copy.start()

    def stage3(i):
        p = lax.rem(i, RING)
        for copy in send2(i):
            copy.wait()
        quad[p, 0] = part[p, 0, x] + (r2[p, 0] + r2[p, 1])
        quad[p, 1] = part[p, 1, :, y] + (r2[p, 2] + r2[p, 3])
        for copy in send3(i):
            copy.start()

    def stage4(i):
        p = lax.rem(i, RING)
        for copy in send3(i):
            copy.wait()
        quad[p, 1, xp, pl.ds(0, QUART)] += r3[p, 0]
        quad[p, 1, xm, pl.ds(QUART, QUART)] += r3[p, 1]
        quad[p, 0, yp, pl.ds(0, QUART)] += r3[p, 2]
        quad[p, 0, ym, pl.ds(QUART, QUART)] += r3[p, 3]
        for copy in send4(i):
            copy.start()

    def stage5(i):
        p = lax.rem(i, RING)
        for copy in send4(i):
            copy.wait()
        done[i, :, pl.ds(0, LANES)] = quad[p, 0, y] + (r4[p, 2] + r4[p, 3])
        done[i, :, pl.ds(LANES, LANES)] = quad[p, 1, x] + (r4[p, 0] + r4[p, 1])

        @pl.when(i > Z_BEGIN - 4)
        def _():
            zsend(i).start()

    def step(i, carry):
        pl.when(jnp.logical_and(lax.rem(i, PER) == PER - 1, i < STEPS - PER))(functools.partial(fetch, i))
        for lag, stage in enumerate((stage1, stage2, stage3, stage4, stage5)):
            pl.when(jnp.logical_and(i >= lag, i < STEPS + lag))(functools.partial(stage, i - lag))

        @pl.when(i == Z_BEGIN)
        def _():
            def begin(j, carry):
                zsend(j).start()
                return carry

            lax.fori_loop(PER, Z_BEGIN - 3, begin, 0)

        return carry

    lax.fori_loop(0, STEPS + 4, step, 0)

    def gather(i, carry):
        zsend(i).wait()
        h = lax.rem(i, PER)
        done[h] += zr[i // PER, h]
        return carry

    lax.fori_loop(PER, STEPS, gather, 0)
    for h in range(PER):
        out[:, pl.ds(h * SUB, SUB)] = done[h].T
    a_swap.wait_send()
    for k in range(1, NZ):
        forward(k).wait_send()
    for k in range(1, NZ - 1):
        a_send(k).wait_send()
    for half in range(2):
        leg1(half).wait_send()
        leg2(half).wait_send()


def ladder_of(amplitudes, integrals, block_sizes):
    f32, bf16 = jnp.float32, jnp.bfloat16
    dma = pltpu.SemaphoreType.DMA
    scratch = [
        pltpu.VMEM((NZ, ROWS, KD), f32),
        pltpu.VMEM((NZ, ROWS, KD), f32),
        pltpu.VMEM((2, ROWS // 2, KD), f32),
        pltpu.VMEM((PER, NX * NX, SUB, KD), f32),
        pltpu.VMEM((PER, NX * NX, SUB, KD), f32),
        pltpu.VMEM((ROWS, 6 * KD), bf16),
        pltpu.VMEM((PER, NX * NX * SUB, 6 * KD), bf16),
        pltpu.VMEM((RING, 2, NX, NX, SUB, LANES), f32),
        pltpu.VMEM((RING, 2, NX, SUB, LANES), f32),
        pltpu.VMEM((STEPS, SUB, ROWS), f32),
        pltpu.VMEM((RING, 4, NX, QUART, LANES), f32),
        pltpu.VMEM((RING, 4, NX, SUB, LANES), f32),
        pltpu.VMEM((RING, 4, QUART, LANES), f32),
        pltpu.VMEM((RING, 4, SUB, LANES), f32),
        pltpu.VMEM((NZ, PER, SUB, ROWS), f32),
        dma, dma((PER,)), dma((PER,)), dma((PER,)),
        dma((NZ,)), dma((NZ,)), dma((4,)), dma((4,)), dma((NZ,)), dma((NZ,)),
        dma((RING, 4)), dma((RING, 4)), dma((RING, 4)), dma((RING, 4)),
        dma((RING, 4)), dma((RING, 4)), dma((RING, 4)), dma((RING, 4)),
        dma((STEPS,)), dma((STEPS,)),
    ]
    return pl.pallas_call(
        ladder_kernel,
        out_shape=jax.ShapeDtypeStruct((ROWS, COLS), f32),
        in_specs=[
            pl.BlockSpec(memory_space=pltpu.SMEM),
            pl.BlockSpec(memory_space=pl.ANY),
            pl.BlockSpec(memory_space=pl.ANY),
        ],
        out_specs=pl.BlockSpec(memory_space=pltpu.VMEM),
        scratch_shapes=scratch,
        compiler_params=pltpu.CompilerParams(
            collective_id=0, has_side_effects=True, vmem_limit_bytes=52 * 1024 * 1024
        ),
        cost_estimate=pl.CostEstimate(
            flops=3 * 2 * 2048 * 2048 * 768, bytes_accessed=12 * 1024 * 1024, transcendentals=0
        ),
        name="ladder",
    )(block_sizes, amplitudes, integrals.reshape(NX * NX, 2, COLS, KD))


def lookup(table, indices):
    entries = jnp.arange(table.shape[0], dtype=jnp.int32)
    hits = indices[:, None] == entries[None, :]
    return jnp.sum(jnp.where(hits, table[None, :], jnp.zeros((), table.dtype)), axis=1)


def body(
    amplitudes,
    integrals,
    driver,
    block_sizes,
    pair_first,
    pair_second,
    ab_first,
    ab_second,
    occ_energy,
    virt_energy,
):
    ladder = ladder_of(amplitudes, integrals, block_sizes)
    occupied = lookup(occ_energy, pair_first) + lookup(occ_energy, pair_second)
    denominator = (
        occupied[:, None]
        - lookup(virt_energy, ab_first)[None, :]
        - lookup(virt_energy, ab_second)[None, :]
    )
    return (driver + ladder) / denominator


def solution(mesh):
    placed = (
        P("pair", "slab"),
        P(None, ("slab", "pair")),
        P("pair", "slab"),
        P(),
        P("pair"),
        P("pair"),
        P("slab"),
        P("slab"),
        P(),
        P(),
    )
    return jax.shard_map(
        body, mesh=mesh, in_specs=placed, out_specs=P("pair", "slab"), check_vma=False
    )
```

```python
import functools

import jax
import jax.numpy as jnp
from jax import lax
from jax.experimental import pallas as pl
from jax.experimental.pallas import tpu as pltpu
from jax.sharding import PartitionSpec as P

MESH = pl.DeviceIdType.MESH
NT = (((1,), (1,)), ((), ()))

NZ = 8
NX = 4
ROWS = 256
KD = 384
COLS = 128
SUB = 64
PER = COLS // SUB
QUART = SUB // 2
STEPS = NZ * PER
LANES = 128
MROWS = 2 * NX * SUB
RING = 4
ORDER = (0, 7, 6, 2, 3, 5, 4, 1)
FAR = ORDER.index(4)
FIRST = (1, 2, 3)
A_BEGIN = ((0, (4,)), (2, (5,)), (5, (7,)))
LEG1_BEGIN = 5
LEG2_BEGIN = 8
Z_BEGIN = 14
Z_END = STEPS + 2


def split(v):
    hi = v.astype(jnp.bfloat16)
    lo = (v - hi.astype(jnp.float32)).astype(jnp.bfloat16)
    return hi, lo


def ladder_kernel(
    sizes_hbm, a_hbm, b_hbm, pf_hbm, ps_hbm, af_hbm, as_hbm, occ_hbm, virt_hbm, drive_hbm, out,
    drive, drive_sem, denominator, sizes, pf, ps, af, asec, occ, virt, small_sem, a_own, a_sib, relay, b_own, b_sib, a3, b3, part, quad, done,
    r1, r2, r3, r4, mg, mh, fin,
    loc_sem, bl, bs, br, as_, ar, hs, hr, fs, fr, s1, q1, s2, q2, s3, q3, s4, q4, zs, zq, es, eq,
):
    z = lax.axis_index("pair")
    s = lax.axis_index("slab")
    x, y, c = s // (2 * NX), (s // 2) % NX, s % 2

    def slab(xx, yy, cc):
        return (xx * NX + yy) * 2 + cc

    def up(v, n, d):
        return lax.rem(v + d, n)

    xp, xo, xm = up(x, NX, 1), up(x, NX, 2), up(x, NX, 3)
    yp, yo, ym = up(y, NX, 1), up(y, NX, 2), up(y, NX, 3)
    sibling = (z, slab(x, y, 1 - c))
    side = ((z, slab(xp, y, c)), (z, slab(xm, y, c)), (z, slab(x, yp, c)), (z, slab(x, ym, c)))

    def zdev(d):
        return (up(z, NZ, d), s)

    def remote(src, dst, send, recv, dev):
        return pltpu.make_async_remote_copy(
            src_ref=src, dst_ref=dst, send_sem=send, recv_sem=recv, device_id=dev, device_id_type=MESH
        )

    barrier = pltpu.get_barrier_semaphore()
    peers = [sibling, *side] + [zdev(d) for d in range(1, NZ)]
    for dev in peers:
        pl.semaphore_signal(barrier, inc=1, device_id=dev, device_id_type=MESH)
    pl.semaphore_wait(barrier, len(peers))

    small = ((sizes_hbm, sizes), (pf_hbm, pf), (ps_hbm, ps), (af_hbm, af), (as_hbm, asec), (occ_hbm, occ), (virt_hbm, virt))
    small = [pltpu.make_async_copy(src, dst, small_sem.at[n]) for n, (src, dst) in enumerate(small)]

    def acols(d):
        return pl.ds(pl.multiple_of(up(z, NZ, d) * KD, KD), KD)

    def b_load(h):
        return pltpu.make_async_copy(b_hbm.at[:, c, pl.ds(h * SUB, SUB)], b_own.at[h], bl.at[h])

    def b_swap(h):
        return remote(b_hbm.at[:, 1 - c, pl.ds(h * SUB, SUB)], b_sib.at[h], bs.at[h], br.at[h], sibling)

    a_loc = pltpu.make_async_copy(a_hbm.at[:, acols(0)], a_own.at[0], loc_sem)
    a_swap = remote(a_hbm.at[:, acols(0)], a_sib.at[0], fs.at[0], fr.at[0], sibling)
    b_swap(0).start()
    b_load(0).start()
    a_swap.start()
    a_loc.start()
    for copy in small:
        copy.start()
    for h in range(1, PER):
        b_swap(h).start()
        b_load(h).start()

    def a_send(k):
        d = NZ - ORDER[k]
        return remote(a_hbm.at[:, acols(d)], a_own.at[k], as_.at[k], ar.at[k], zdev(d))

    def leg1(h):
        rows = pl.ds(h * (ROWS // 2), ROWS // 2)
        return remote(a_hbm.at[rows, acols(4)], relay.at[h], hs.at[h], hr.at[h], zdev((2, 6)[h]))

    def leg2(h):
        rows = pl.ds(h * (ROWS // 2), ROWS // 2)
        return remote(relay.at[h], a_own.at[FAR, rows], hs.at[2 + h], hr.at[2 + h], zdev((2, 6)[h]))

    def forward(k):
        return remote(a_own.at[k], a_sib.at[k], fs.at[k], fr.at[k], sibling)

    drive_copy = pltpu.make_async_copy(drive_hbm, drive, drive_sem)
    drive_copy.start()
    for k in FIRST:
        a_send(k).start()
    small[0].wait()

    limit = sizes[s // 4]
    column = lax.broadcasted_iota(jnp.int32, (SUB, KD), 1)

    def convert(src, h, first, slab_at):
        live = column < limit - (slab_at % 4) * (NZ * KD) - z * KD

        def one(j, carry):
            hi, lo = split(jnp.where(live, src[h, j], 0.0))
            rows = pl.ds(pl.multiple_of(j * SUB, SUB), SUB)
            b3[h, rows, pl.ds(first, KD)] = hi
            b3[h, rows, pl.ds(2 * KD + first, KD)] = lo
            b3[h, rows, pl.ds(4 * KD + first, KD)] = hi
            return carry

        lax.fori_loop(0, NX * NX, one, 0)

    def send1(i):
        p = lax.rem(i, RING)
        src = (
            part.at[p, 0, xo, :, pl.ds(0, QUART)],
            part.at[p, 0, xo, :, pl.ds(QUART, QUART)],
            part.at[p, 1, :, yo, pl.ds(0, QUART)],
            part.at[p, 1, :, yo, pl.ds(QUART, QUART)],
        )
        return [remote(src[k], r1.at[p, k], s1.at[p, k], q1.at[p, k], side[k]) for k in range(4)]

    def send2(i):
        p = lax.rem(i, RING)
        src = (part.at[p, 0, xp], part.at[p, 0, xm], part.at[p, 1, :, yp], part.at[p, 1, :, ym])
        return [remote(src[k], r2.at[p, k], s2.at[p, k], q2.at[p, k], side[k]) for k in range(4)]

    def send3(i):
        p = lax.rem(i, RING)
        src = (
            quad.at[p, 1, xo, pl.ds(0, QUART)],
            quad.at[p, 1, xo, pl.ds(QUART, QUART)],
            quad.at[p, 0, yo, pl.ds(0, QUART)],
            quad.at[p, 0, yo, pl.ds(QUART, QUART)],
        )
        return [remote(src[k], r3.at[p, k], s3.at[p, k], q3.at[p, k], side[k]) for k in range(4)]

    def send4(i):
        p = lax.rem(i, RING)
        src = (quad.at[p, 1, xp], quad.at[p, 1, xm], quad.at[p, 0, yp], quad.at[p, 0, ym])
        return [remote(src[k], r4.at[p, k], s4.at[p, k], q4.at[p, k], side[k]) for k in range(4)]

    def zparts(k):
        return range(2 if k == FAR else 1)

    def zsend(k, h, part_at):
        d, i = ORDER[k], k * PER + h
        if d == 4:
            src, dst, dev = done.at[i, pl.ds(part_at * QUART, QUART)], mh.at[part_at, h], zdev(3 + 2 * part_at)
        elif d < 4:
            src, dst, dev = done.at[i], mg.at[0, d - 2, h], zdev(d - 1)
        else:
            src, dst, dev = done.at[i], mg.at[1, 6 - d, h], zdev(d + 1)
        return remote(src, dst, zs.at[k, h, part_at], zq.at[k, h, part_at], dev)

    def zstart(i):
        for k, d in enumerate(ORDER):
            if d not in (0, 1, 7):
                @pl.when(i // PER == k)
                def _():
                    for n in zparts(k):
                        zsend(k, lax.rem(i, PER), n).start()

    def last(n, h):
        i = ORDER.index((1, 7)[n]) * PER + h
        return remote(done.at[i], fin.at[n, h], es.at[n, h], eq.at[n, h], zdev((1, 7)[n]))

    def merge(n, h):
        for d in ((2, 3), (6, 5))[n]:
            zsend(ORDER.index(d), h, 0).wait_recv()
        zsend(FAR, h, n).wait_recv()
        i = ORDER.index((1, 7)[n]) * PER + h
        done[i] += mg[n, 0, h] + mg[n, 1, h]
        done[i, pl.ds(n * QUART, QUART)] += mh[n, h]
        last(n, h).start()

    def ready(n, h):
        return ORDER.index((1, 7)[n]) * PER + h + 4 <= Z_END

    def stage1(i):
        p = lax.rem(i, RING)
        k = i // PER
        h = lax.rem(i, PER)

        for step_at in range(PER):
            @pl.when(i == step_at)
            def _():
                b_load(step_at).wait()
                convert(b_own, step_at, 0, s)
                if step_at == 0:
                    a_loc.wait()
                b_swap(step_at).wait()
                convert(b_sib, step_at, KD, slab(x, y, 1 - c))

        @pl.when(h == 0)
        def _():
            forward(k).wait_recv()
            for first, source in ((0, a_own), (KD, a_sib)):
                hi, lo = split(source[k])
                a3[:, pl.ds(first, KD)] = hi
                a3[:, pl.ds(2 * KD + first, KD)] = hi
                a3[:, pl.ds(4 * KD + first, KD)] = lo

        def columns(m, carry):
            rows = pl.ds(pl.multiple_of(m * MROWS, MROWS), MROWS)
            acc = lax.dot_general(b3[h, rows, :], a3[...], NT, preferred_element_type=jnp.float32)
            for xx in range(2):
                for yy in range(NX):
                    at = (xx * NX + yy) * SUB
                    for half in range(2):
                        part[p, half, 2 * m + xx, yy] = acc[at:at + SUB, half * LANES:(half + 1) * LANES]
            return carry

        lax.fori_loop(0, NX // 2, columns, 0)
        for copy in send1(i):
            copy.start()

        for begin, blocks in A_BEGIN:
            @pl.when(i == begin)
            def _():
                for kk in blocks:
                    a_send(kk).start()

        @pl.when(i == LEG1_BEGIN)
        def _():
            for half in range(2):
                leg1(half).start()

    def fetch(i):
        k = i // PER

        @pl.when(k + 1 != FAR)
        def _():
            a_wait = remote(a_own.at[k + 1], a_own.at[k + 1], as_.at[k + 1], ar.at[k + 1], sibling)
            a_wait.wait_recv()

        @pl.when(k + 1 == FAR)
        def _():
            for half in range(2):
                leg2(half).wait_recv()

        forward(k + 1).start()

    def stage2(i):
        p = lax.rem(i, RING)
        for copy in send1(i):
            copy.wait()
        part[p, 0, xp, :, pl.ds(0, QUART)] += r1[p, 0]
        part[p, 0, xm, :, pl.ds(QUART, QUART)] += r1[p, 1]
        part[p, 1, :, yp, pl.ds(0, QUART)] += r1[p, 2]
        part[p, 1, :, ym, pl.ds(QUART, QUART)] += r1[p, 3]
        for copy in send2(i):
            copy.start()

    def stage3(i):
        p = lax.rem(i, RING)
        for copy in send2(i):
            copy.wait()
        quad[p, 0] = part[p, 0, x] + (r2[p, 0] + r2[p, 1])
        quad[p, 1] = part[p, 1, :, y] + (r2[p, 2] + r2[p, 3])
        for copy in send3(i):
            copy.start()

    def stage4(i):
        p = lax.rem(i, RING)
        for copy in send3(i):
            copy.wait()
        quad[p, 1, xp, pl.ds(0, QUART)] += r3[p, 0]
        quad[p, 1, xm, pl.ds(QUART, QUART)] += r3[p, 1]
        quad[p, 0, yp, pl.ds(0, QUART)] += r3[p, 2]
        quad[p, 0, ym, pl.ds(QUART, QUART)] += r3[p, 3]
        for copy in send4(i):
            copy.start()

    def stage5(i):
        p = lax.rem(i, RING)
        for copy in send4(i):
            copy.wait()
        done[i, :, pl.ds(0, LANES)] = quad[p, 0, y] + (r4[p, 2] + r4[p, 3])
        done[i, :, pl.ds(LANES, LANES)] = quad[p, 1, x] + (r4[p, 0] + r4[p, 1])

        @pl.when(i > Z_BEGIN - 4)
        def _():
            zstart(i)

    def looked_up(table, index, width):
        entry = lax.broadcasted_iota(jnp.int32, (table.shape[1], width), 0)
        hits = jnp.where(entry == index[...], 1.0, 0.0)
        row = jnp.broadcast_to(table[...], (8, table.shape[1]))
        return lax.dot_general(
            row, hits, (((1,), (0,)), ((), ())), precision=lax.Precision.HIGHEST, preferred_element_type=jnp.float32
        )[0:1]

    def energies():
        for copy in small[1:]:
            copy.wait()
        occupied = looked_up(occ, pf, ROWS) + looked_up(occ, ps, ROWS)
        rows = jnp.broadcast_to(occupied, (COLS, ROWS)).T
        first, second = looked_up(virt, af, COLS), looked_up(virt, asec, COLS)
        denominator[...] = (rows - first) - second

    def step(i, carry):
        pl.when(jnp.logical_and(lax.rem(i, PER) == PER - 1, i < STEPS - PER))(functools.partial(fetch, i))
        for lag, stage in enumerate((stage1, stage2, stage3, stage4, stage5)):
            pl.when(jnp.logical_and(i >= lag, i < STEPS + lag))(functools.partial(stage, i - lag))

        pl.when(i == PER)(energies)

        @pl.when(i == LEG2_BEGIN)
        def _():
            for half in range(2):
                leg1(half).wait_recv()
                leg2(half).start()

        @pl.when(i == Z_BEGIN)
        def _():
            def begin(j, carry):
                zstart(j)
                return carry

            lax.fori_loop(PER, Z_BEGIN - 3, begin, 0)

        @pl.when(i == Z_END)
        def _():
            for n in range(2):
                for h in range(PER):
                    if ready(n, h):
                        merge(n, h)

        return carry

    lax.fori_loop(0, STEPS + 4, step, 0)

    for n in range(2):
        for h in range(PER):
            if not ready(n, h):
                merge(n, h)
    drive_copy.wait()
    for h in range(PER):
        for n in range(2):
            last(n, h).wait_recv()
        cols = pl.ds(h * SUB, SUB)
        ladder = (done[h] + (fin[0, h] + fin[1, h])).T
        out[:, cols] = (drive[:, cols] + ladder) / denominator[:, cols]
    for n in range(2):
        for h in range(PER):
            last(n, h).wait_send()
    for k, d in enumerate(ORDER):
        if d not in (0, 1, 7):
            for h in range(PER):
                for n in zparts(k):
                    zsend(k, h, n).wait_send()
    a_swap.wait_send()
    for k in range(1, NZ):
        forward(k).wait_send()
    for k in range(1, NZ):
        if k != FAR:
            a_send(k).wait_send()
    for half in range(2):
        leg1(half).wait_send()
        leg2(half).wait_send()


def update(amplitudes, integrals, driver, block_sizes, *tables):
    f32, bf16 = jnp.float32, jnp.bfloat16
    dma = pltpu.SemaphoreType.DMA
    scratch = [
        pltpu.VMEM((ROWS, COLS), f32), dma, pltpu.VMEM((ROWS, COLS), f32),
        pltpu.SMEM((NZ,), jnp.int32),
        *(pltpu.VMEM(table.shape, table.dtype) for table in tables),
        dma((len(tables) + 1,)),
        pltpu.VMEM((NZ, ROWS, KD), f32),
        pltpu.VMEM((NZ, ROWS, KD), f32),
        pltpu.VMEM((2, ROWS // 2, KD), f32),
        pltpu.VMEM((PER, NX * NX, SUB, KD), f32),
        pltpu.VMEM((PER, NX * NX, SUB, KD), f32),
        pltpu.VMEM((ROWS, 6 * KD), bf16),
        pltpu.VMEM((PER, NX * NX * SUB, 6 * KD), bf16),
        pltpu.VMEM((RING, 2, NX, NX, SUB, LANES), f32),
        pltpu.VMEM((RING, 2, NX, SUB, LANES), f32),
        pltpu.VMEM((STEPS, SUB, ROWS), f32),
        pltpu.VMEM((RING, 4, NX, QUART, LANES), f32),
        pltpu.VMEM((RING, 4, NX, SUB, LANES), f32),
        pltpu.VMEM((RING, 4, QUART, LANES), f32),
        pltpu.VMEM((RING, 4, SUB, LANES), f32),
        pltpu.VMEM((2, 2, PER, SUB, ROWS), f32),
        pltpu.VMEM((2, PER, QUART, ROWS), f32),
        pltpu.VMEM((2, PER, SUB, ROWS), f32),
        dma, dma((PER,)), dma((PER,)), dma((PER,)),
        dma((NZ,)), dma((NZ,)), dma((4,)), dma((4,)), dma((NZ,)), dma((NZ,)),
        dma((RING, 4)), dma((RING, 4)), dma((RING, 4)), dma((RING, 4)),
        dma((RING, 4)), dma((RING, 4)), dma((RING, 4)), dma((RING, 4)),
        dma((NZ, PER, 2)), dma((NZ, PER, 2)), dma((2, PER)), dma((2, PER)),
    ]
    return pl.pallas_call(
        ladder_kernel,
        out_shape=jax.ShapeDtypeStruct((ROWS, COLS), f32),
        in_specs=[pl.BlockSpec(memory_space=pltpu.HBM)] * (4 + len(tables)),
        out_specs=pl.BlockSpec(memory_space=pltpu.VMEM),
        scratch_shapes=scratch,
        compiler_params=pltpu.CompilerParams(
            collective_id=0, has_side_effects=True, vmem_limit_bytes=60 * 1024 * 1024
        ),
        cost_estimate=pl.CostEstimate(
            flops=3 * 2 * 2048 * 2048 * 768, bytes_accessed=12 * 1024 * 1024, transcendentals=0
        ),
        name="ladder",
    )(block_sizes, amplitudes, integrals.reshape(NX * NX, 2, COLS, KD), *tables, driver)


def body(
    amplitudes,
    integrals,
    driver,
    block_sizes,
    pair_first,
    pair_second,
    ab_first,
    ab_second,
    occ_energy,
    virt_energy,
):
    tables = (pair_first, pair_second, ab_first, ab_second, occ_energy, virt_energy)
    return update(amplitudes, integrals, driver, block_sizes, *(table[None] for table in tables))


def solution(mesh):
    placed = (
        P("pair", "slab"),
        P(None, ("slab", "pair")),
        P("pair", "slab"),
        P(),
        P("pair"),
        P("pair"),
        P("slab"),
        P("slab"),
        P(),
        P(),
    )
    return jax.shard_map(
        body, mesh=mesh, in_specs=placed, out_specs=P("pair", "slab"), check_vma=False
    )
```

```python
import functools

import jax
import jax.numpy as jnp
from jax import lax
from jax.experimental import pallas as pl
from jax.experimental.pallas import tpu as pltpu
from jax.sharding import PartitionSpec as P

MESH = pl.DeviceIdType.MESH
NT = (((1,), (1,)), ((), ()))

NZ = 8
NX = 4
ROWS = 256
KD = 384
COLS = 128
SUB = 64
PER = COLS // SUB
QUART = SUB // 2
STEPS = NZ * PER
LANES = 128
MROWS = 2 * NX * SUB
RING = 4
ORDER = (0, 7, 6, 2, 3, 5, 4, 1)
FAR = ORDER.index(4)
FIRST = (1, 2, 3)
A_BEGIN = ((0, (4,)), (2, (5,)), (5, (7,)))
LEG1_BEGIN = 5
LEG2_BEGIN = 8
Z_BEGIN = 14
Z_END = STEPS + 2


def split(v):
    hi = v.astype(jnp.bfloat16)
    lo = (v - hi.astype(jnp.float32)).astype(jnp.bfloat16)
    return hi, lo


def ladder_kernel(
    sizes_hbm, a_hbm, b_hbm, pf_hbm, ps_hbm, af_hbm, as_hbm, occ_hbm, virt_hbm, drive_hbm, out,
    drive, drive_sem, denominator, sizes, pf, ps, af, asec, occ, virt, small_sem, a_own, a_sib, relay, b_own, b_sib, a3, b3, part, quad, done,
    r1, r2, r3, r4, mg, mh, fin,
    loc_sem, bl, bs, br, as_, ar, hs, hr, fs, fr, s1, q1, s2, q2, s3, q3, s4, q4, zs, zq, es, eq,
):
    z = lax.axis_index("pair")
    s = lax.axis_index("slab")
    x, y, c = s // (2 * NX), (s // 2) % NX, s % 2

    def slab(xx, yy, cc):
        return (xx * NX + yy) * 2 + cc

    def up(v, n, d):
        return lax.rem(v + d, n)

    xp, xo, xm = up(x, NX, 1), up(x, NX, 2), up(x, NX, 3)
    yp, yo, ym = up(y, NX, 1), up(y, NX, 2), up(y, NX, 3)
    sibling = (z, slab(x, y, 1 - c))
    side = ((z, slab(xp, y, c)), (z, slab(xm, y, c)), (z, slab(x, yp, c)), (z, slab(x, ym, c)))

    def zdev(d):
        return (up(z, NZ, d), s)

    def remote(src, dst, send, recv, dev):
        return pltpu.make_async_remote_copy(
            src_ref=src, dst_ref=dst, send_sem=send, recv_sem=recv, device_id=dev, device_id_type=MESH
        )

    barrier = pltpu.get_barrier_semaphore()
    peers = [sibling, *side] + [zdev(d) for d in range(1, NZ)]
    for dev in peers:
        pl.semaphore_signal(barrier, inc=1, device_id=dev, device_id_type=MESH)

    small = ((sizes_hbm, sizes), (pf_hbm, pf), (ps_hbm, ps), (af_hbm, af), (as_hbm, asec), (occ_hbm, occ), (virt_hbm, virt))
    small = [pltpu.make_async_copy(src, dst, small_sem.at[n]) for n, (src, dst) in enumerate(small)]

    def acols(d):
        return pl.ds(pl.multiple_of(up(z, NZ, d) * KD, KD), KD)

    def b_load(h):
        return pltpu.make_async_copy(b_hbm.at[:, c, pl.ds(h * SUB, SUB)], b_own.at[h], bl.at[h])

    def b_swap(h):
        return remote(b_hbm.at[:, 1 - c, pl.ds(h * SUB, SUB)], b_sib.at[h], bs.at[h], br.at[h], sibling)

    a_loc = pltpu.make_async_copy(a_hbm.at[:, acols(0)], a_own.at[0], loc_sem)
    a_swap = remote(a_hbm.at[:, acols(0)], a_sib.at[0], fs.at[0], fr.at[0], sibling)
    drive_copy = pltpu.make_async_copy(drive_hbm, drive, drive_sem)
    for copy in small:
        copy.start()
    b_load(0).start()
    a_loc.start()
    pl.semaphore_wait(barrier, len(peers))
    b_swap(0).start()
    a_swap.start()

    def a_send(k):
        d = NZ - ORDER[k]
        return remote(a_hbm.at[:, acols(d)], a_own.at[k], as_.at[k], ar.at[k], zdev(d))

    def leg1(h):
        rows = pl.ds(h * (ROWS // 2), ROWS // 2)
        return remote(a_hbm.at[rows, acols(4)], relay.at[h], hs.at[h], hr.at[h], zdev((2, 6)[h]))

    def leg2(h):
        rows = pl.ds(h * (ROWS // 2), ROWS // 2)
        return remote(relay.at[h], a_own.at[FAR, rows], hs.at[2 + h], hr.at[2 + h], zdev((2, 6)[h]))

    def forward(k):
        return remote(a_own.at[k], a_sib.at[k], fs.at[k], fr.at[k], sibling)

    for k in FIRST:
        a_send(k).start()
    for h in range(1, PER):
        b_swap(h).start()
        b_load(h).start()
    drive_copy.start()
    small[0].wait()

    def looked_up(table, index, width):
        entry = lax.broadcasted_iota(jnp.int32, (table.shape[1], width), 0)
        hits = jnp.where(entry == index[...], 1.0, 0.0).astype(jnp.bfloat16)
        row = jnp.broadcast_to(table[...], (8, table.shape[1]))
        hi = row.astype(jnp.bfloat16).astype(jnp.float32)
        mid = (row - hi).astype(jnp.bfloat16).astype(jnp.float32)
        term = lax.broadcasted_iota(jnp.int32, row.shape, 0)
        terms = jnp.where(term == 0, hi, jnp.where(term == 1, mid, row - hi - mid)).astype(jnp.bfloat16)
        got = lax.dot_general(terms, hits, (((1,), (0,)), ((), ())), preferred_element_type=jnp.float32)
        return got[0:1] + (got[1:2] + got[2:3])

    def energies():
        for copy in small[1:]:
            copy.wait()
        occupied = looked_up(occ, pf, ROWS) + looked_up(occ, ps, ROWS)
        rows = jnp.broadcast_to(occupied, (COLS, ROWS)).T
        first, second = looked_up(virt, af, COLS), looked_up(virt, asec, COLS)
        denominator[...] = (rows - first) - second

    energies()

    limit = sizes[s // 4]
    column = lax.broadcasted_iota(jnp.int32, (SUB, KD), 1)

    def convert(src, h, first, slab_at):
        live = column < limit - (slab_at % 4) * (NZ * KD) - z * KD

        def one(j, carry):
            hi, lo = split(jnp.where(live, src[h, j], 0.0))
            rows = pl.ds(pl.multiple_of(j * SUB, SUB), SUB)
            b3[h, rows, pl.ds(first, KD)] = hi
            b3[h, rows, pl.ds(2 * KD + first, KD)] = lo
            b3[h, rows, pl.ds(4 * KD + first, KD)] = hi
            return carry

        lax.fori_loop(0, NX * NX, one, 0)

    def send1(i):
        p = lax.rem(i, RING)
        src = (
            part.at[p, 0, xo, :, pl.ds(0, QUART)],
            part.at[p, 0, xo, :, pl.ds(QUART, QUART)],
            part.at[p, 1, :, yo, pl.ds(0, QUART)],
            part.at[p, 1, :, yo, pl.ds(QUART, QUART)],
        )
        return [remote(src[k], r1.at[p, k], s1.at[p, k], q1.at[p, k], side[k]) for k in range(4)]

    def send2(i):
        p = lax.rem(i, RING)
        src = (part.at[p, 0, xp], part.at[p, 0, xm], part.at[p, 1, :, yp], part.at[p, 1, :, ym])
        return [remote(src[k], r2.at[p, k], s2.at[p, k], q2.at[p, k], side[k]) for k in range(4)]

    def send3(i):
        p = lax.rem(i, RING)
        src = (
            quad.at[p, 1, xo, pl.ds(0, QUART)],
            quad.at[p, 1, xo, pl.ds(QUART, QUART)],
            quad.at[p, 0, yo, pl.ds(0, QUART)],
            quad.at[p, 0, yo, pl.ds(QUART, QUART)],
        )
        return [remote(src[k], r3.at[p, k], s3.at[p, k], q3.at[p, k], side[k]) for k in range(4)]

    def send4(i):
        p = lax.rem(i, RING)
        src = (quad.at[p, 1, xp], quad.at[p, 1, xm], quad.at[p, 0, yp], quad.at[p, 0, ym])
        return [remote(src[k], r4.at[p, k], s4.at[p, k], q4.at[p, k], side[k]) for k in range(4)]

    def zparts(k):
        return range(2 if k == FAR else 1)

    def zsend(k, h, part_at):
        d, i = ORDER[k], k * PER + h
        if d == 4:
            src, dst, dev = done.at[i, pl.ds(part_at * QUART, QUART)], mh.at[part_at, h], zdev(3 + 2 * part_at)
        elif d < 4:
            src, dst, dev = done.at[i], mg.at[0, d - 2, h], zdev(d - 1)
        else:
            src, dst, dev = done.at[i], mg.at[1, 6 - d, h], zdev(d + 1)
        return remote(src, dst, zs.at[k, h, part_at], zq.at[k, h, part_at], dev)

    def zstart(i):
        for k, d in enumerate(ORDER):
            if d not in (0, 1, 7):
                @pl.when(i // PER == k)
                def _():
                    for n in zparts(k):
                        zsend(k, lax.rem(i, PER), n).start()

    def last(n, h):
        i = ORDER.index((1, 7)[n]) * PER + h
        return remote(done.at[i], fin.at[n, h], es.at[n, h], eq.at[n, h], zdev((1, 7)[n]))

    def merge(n, h):
        for d in ((2, 3), (6, 5))[n]:
            zsend(ORDER.index(d), h, 0).wait_recv()
        zsend(FAR, h, n).wait_recv()
        i = ORDER.index((1, 7)[n]) * PER + h
        done[i] += mg[n, 0, h] + mg[n, 1, h]
        done[i, pl.ds(n * QUART, QUART)] += mh[n, h]
        last(n, h).start()

    def ready(n, h):
        return ORDER.index((1, 7)[n]) * PER + h + 4 <= Z_END

    def stage1(i):
        p = lax.rem(i, RING)
        k = i // PER
        h = lax.rem(i, PER)

        for step_at in range(PER):
            @pl.when(i == step_at)
            def _():
                b_load(step_at).wait()
                convert(b_own, step_at, 0, s)
                if step_at == 0:
                    a_loc.wait()
                b_swap(step_at).wait()
                convert(b_sib, step_at, KD, slab(x, y, 1 - c))

        @pl.when(h == 0)
        def _():
            forward(k).wait_recv()
            for first, source in ((0, a_own), (KD, a_sib)):
                hi, lo = split(source[k])
                a3[:, pl.ds(first, KD)] = hi
                a3[:, pl.ds(2 * KD + first, KD)] = hi
                a3[:, pl.ds(4 * KD + first, KD)] = lo

        def columns(m, carry):
            rows = pl.ds(pl.multiple_of(m * MROWS, MROWS), MROWS)
            acc = lax.dot_general(b3[h, rows, :], a3[...], NT, preferred_element_type=jnp.float32)
            for xx in range(2):
                for yy in range(NX):
                    at = (xx * NX + yy) * SUB
                    for half in range(2):
                        part[p, half, 2 * m + xx, yy] = acc[at:at + SUB, half * LANES:(half + 1) * LANES]
            return carry

        lax.fori_loop(0, NX // 2, columns, 0)
        for copy in send1(i):
            copy.start()

        for begin, blocks in A_BEGIN:
            @pl.when(i == begin)
            def _():
                for kk in blocks:
                    a_send(kk).start()

        @pl.when(i == LEG1_BEGIN)
        def _():
            for half in range(2):
                leg1(half).start()

    def fetch(i):
        k = i // PER

        @pl.when(k + 1 != FAR)
        def _():
            a_wait = remote(a_own.at[k + 1], a_own.at[k + 1], as_.at[k + 1], ar.at[k + 1], sibling)
            a_wait.wait_recv()

        @pl.when(k + 1 == FAR)
        def _():
            for half in range(2):
                leg2(half).wait_recv()

        forward(k + 1).start()

    def stage2(i):
        p = lax.rem(i, RING)
        for copy in send1(i):
            copy.wait()
        part[p, 0, xp, :, pl.ds(0, QUART)] += r1[p, 0]
        part[p, 0, xm, :, pl.ds(QUART, QUART)] += r1[p, 1]
        part[p, 1, :, yp, pl.ds(0, QUART)] += r1[p, 2]
        part[p, 1, :, ym, pl.ds(QUART, QUART)] += r1[p, 3]
        for copy in send2(i):
            copy.start()

    def stage3(i):
        p = lax.rem(i, RING)
        for copy in send2(i):
            copy.wait()
        quad[p, 0] = part[p, 0, x] + (r2[p, 0] + r2[p, 1])
        quad[p, 1] = part[p, 1, :, y] + (r2[p, 2] + r2[p, 3])
        for copy in send3(i):
            copy.start()

    def stage4(i):
        p = lax.rem(i, RING)
        for copy in send3(i):
            copy.wait()
        quad[p, 1, xp, pl.ds(0, QUART)] += r3[p, 0]
        quad[p, 1, xm, pl.ds(QUART, QUART)] += r3[p, 1]
        quad[p, 0, yp, pl.ds(0, QUART)] += r3[p, 2]
        quad[p, 0, ym, pl.ds(QUART, QUART)] += r3[p, 3]
        for copy in send4(i):
            copy.start()

    def stage5(i):
        p = lax.rem(i, RING)
        for copy in send4(i):
            copy.wait()
        done[i, :, pl.ds(0, LANES)] = quad[p, 0, y] + (r4[p, 2] + r4[p, 3])
        done[i, :, pl.ds(LANES, LANES)] = quad[p, 1, x] + (r4[p, 0] + r4[p, 1])

        @pl.when(i > Z_BEGIN - 4)
        def _():
            zstart(i)

    def step(i, carry):
        pl.when(jnp.logical_and(lax.rem(i, PER) == PER - 1, i < STEPS - PER))(functools.partial(fetch, i))
        for lag, stage in enumerate((stage1, stage2, stage3, stage4, stage5)):
            pl.when(jnp.logical_and(i >= lag, i < STEPS + lag))(functools.partial(stage, i - lag))

        @pl.when(i == LEG2_BEGIN)
        def _():
            for half in range(2):
                leg1(half).wait_recv()
                leg2(half).start()

        @pl.when(i == Z_BEGIN)
        def _():
            def begin(j, carry):
                zstart(j)
                return carry

            lax.fori_loop(PER, Z_BEGIN - 3, begin, 0)

        @pl.when(i == Z_END)
        def _():
            for n in range(2):
                for h in range(PER):
                    if ready(n, h):
                        merge(n, h)

        return carry

    lax.fori_loop(0, STEPS + 4, step, 0)

    for n in range(2):
        for h in range(PER):
            if not ready(n, h):
                merge(n, h)
    drive_copy.wait()
    for h in range(PER):
        for n in range(2):
            last(n, h).wait_recv()
        cols = pl.ds(h * SUB, SUB)
        ladder = (done[h] + (fin[0, h] + fin[1, h])).T
        out[:, cols] = (drive[:, cols] + ladder) / denominator[:, cols]
    for n in range(2):
        for h in range(PER):
            last(n, h).wait_send()
    for k, d in enumerate(ORDER):
        if d not in (0, 1, 7):
            for h in range(PER):
                for n in zparts(k):
                    zsend(k, h, n).wait_send()
    a_swap.wait_send()
    for k in range(1, NZ):
        forward(k).wait_send()
    for k in range(1, NZ):
        if k != FAR:
            a_send(k).wait_send()
    for half in range(2):
        leg1(half).wait_send()
        leg2(half).wait_send()


def update(amplitudes, integrals, driver, block_sizes, *tables):
    f32, bf16 = jnp.float32, jnp.bfloat16
    dma = pltpu.SemaphoreType.DMA
    scratch = [
        pltpu.VMEM((ROWS, COLS), f32), dma, pltpu.VMEM((ROWS, COLS), f32),
        pltpu.SMEM((NZ,), jnp.int32),
        *(pltpu.VMEM(table.shape, table.dtype) for table in tables),
        dma((len(tables) + 1,)),
        pltpu.VMEM((NZ, ROWS, KD), f32),
        pltpu.VMEM((NZ, ROWS, KD), f32),
        pltpu.VMEM((2, ROWS // 2, KD), f32),
        pltpu.VMEM((PER, NX * NX, SUB, KD), f32),
        pltpu.VMEM((PER, NX * NX, SUB, KD), f32),
        pltpu.VMEM((ROWS, 6 * KD), bf16),
        pltpu.VMEM((PER, NX * NX * SUB, 6 * KD), bf16),
        pltpu.VMEM((RING, 2, NX, NX, SUB, LANES), f32),
        pltpu.VMEM((RING, 2, NX, SUB, LANES), f32),
        pltpu.VMEM((STEPS, SUB, ROWS), f32),
        pltpu.VMEM((RING, 4, NX, QUART, LANES), f32),
        pltpu.VMEM((RING, 4, NX, SUB, LANES), f32),
        pltpu.VMEM((RING, 4, QUART, LANES), f32),
        pltpu.VMEM((RING, 4, SUB, LANES), f32),
        pltpu.VMEM((2, 2, PER, SUB, ROWS), f32),
        pltpu.VMEM((2, PER, QUART, ROWS), f32),
        pltpu.VMEM((2, PER, SUB, ROWS), f32),
        dma, dma((PER,)), dma((PER,)), dma((PER,)),
        dma((NZ,)), dma((NZ,)), dma((4,)), dma((4,)), dma((NZ,)), dma((NZ,)),
        dma((RING, 4)), dma((RING, 4)), dma((RING, 4)), dma((RING, 4)),
        dma((RING, 4)), dma((RING, 4)), dma((RING, 4)), dma((RING, 4)),
        dma((NZ, PER, 2)), dma((NZ, PER, 2)), dma((2, PER)), dma((2, PER)),
    ]
    return pl.pallas_call(
        ladder_kernel,
        out_shape=jax.ShapeDtypeStruct((ROWS, COLS), f32),
        in_specs=[pl.BlockSpec(memory_space=pltpu.HBM)] * (4 + len(tables)),
        out_specs=pl.BlockSpec(memory_space=pltpu.VMEM),
        scratch_shapes=scratch,
        compiler_params=pltpu.CompilerParams(
            collective_id=0, has_side_effects=True, vmem_limit_bytes=60 * 1024 * 1024
        ),
        cost_estimate=pl.CostEstimate(
            flops=3 * 2 * 2048 * 2048 * 768, bytes_accessed=12 * 1024 * 1024, transcendentals=0
        ),
        name="ladder",
    )(block_sizes, amplitudes, integrals.reshape(NX * NX, 2, COLS, KD), *tables, driver)


def body(
    amplitudes,
    integrals,
    driver,
    block_sizes,
    pair_first,
    pair_second,
    ab_first,
    ab_second,
    occ_energy,
    virt_energy,
):
    tables = (pair_first, pair_second, ab_first, ab_second, occ_energy, virt_energy)
    return update(amplitudes, integrals, driver, block_sizes, *(table[None] for table in tables))


def solution(mesh):
    placed = (
        P("pair", "slab"),
        P(None, ("slab", "pair")),
        P("pair", "slab"),
        P(),
        P("pair"),
        P("pair"),
        P("slab"),
        P("slab"),
        P(),
        P(),
    )
    return jax.shard_map(
        body, mesh=mesh, in_specs=placed, out_specs=P("pair", "slab"), check_vma=False
    )
```

```python
import functools

import jax
import jax.numpy as jnp
from jax import lax
from jax.experimental import pallas as pl
from jax.experimental.pallas import tpu as pltpu
from jax.sharding import PartitionSpec as P

MESH = pl.DeviceIdType.MESH
NT = (((1,), (1,)), ((), ()))

NZ = 8
NX = 4
ROWS = 256
KD = 384
COLS = 128
SUB = 64
PER = COLS // SUB
QUART = SUB // 2
STEPS = NZ * PER
LANES = 128
MROWS = 2 * NX * SUB
RING = 4
ORDER = (0, 1, 7, 2, 6, 3, 5, 4)
FAR = ORDER.index(4)
FIRST = (1, 2)
A_BEGIN = ((0, (3, 4)), (2, (5, 6)))
LEG1_BEGIN = 4
LEG2_BEGIN = 9
Z_BEGIN = 12
Z_END = STEPS + 2


def split(v):
    hi = v.astype(jnp.bfloat16)
    lo = (v - hi.astype(jnp.float32)).astype(jnp.bfloat16)
    return hi, lo


def ladder_kernel(
    sizes_hbm, a_hbm, b_hbm, pf_hbm, ps_hbm, af_hbm, as_hbm, occ_hbm, virt_hbm, drive_hbm, out,
    drive, drive_sem, denominator, sizes, pf, ps, af, asec, occ, virt, small_sem, a_own, a_sib, relay, b_own, b_sib, a3, b3, part, quad, done,
    r1, r2, r3, r4, mg, mh, fin,
    loc_sem, bl, bs, br, as_, ar, hs, hr, fs, fr, s1, q1, s2, q2, s3, q3, s4, q4, zs, zq, es, eq,
):
    z = lax.axis_index("pair")
    s = lax.axis_index("slab")
    x, y, c = s // (2 * NX), (s // 2) % NX, s % 2

    def slab(xx, yy, cc):
        return (xx * NX + yy) * 2 + cc

    def up(v, n, d):
        return lax.rem(v + d, n)

    xp, xo, xm = up(x, NX, 1), up(x, NX, 2), up(x, NX, 3)
    yp, yo, ym = up(y, NX, 1), up(y, NX, 2), up(y, NX, 3)
    sibling = (z, slab(x, y, 1 - c))
    side = ((z, slab(xp, y, c)), (z, slab(xm, y, c)), (z, slab(x, yp, c)), (z, slab(x, ym, c)))

    def zdev(d):
        return (up(z, NZ, d), s)

    def remote(src, dst, send, recv, dev):
        return pltpu.make_async_remote_copy(
            src_ref=src, dst_ref=dst, send_sem=send, recv_sem=recv, device_id=dev, device_id_type=MESH
        )

    barrier = pltpu.get_barrier_semaphore()
    peers = [sibling, *side] + [zdev(d) for d in range(1, NZ)]
    for dev in peers:
        pl.semaphore_signal(barrier, inc=1, device_id=dev, device_id_type=MESH)

    small = ((sizes_hbm, sizes), (pf_hbm, pf), (ps_hbm, ps), (af_hbm, af), (as_hbm, asec), (occ_hbm, occ), (virt_hbm, virt))
    small = [pltpu.make_async_copy(src, dst, small_sem.at[n]) for n, (src, dst) in enumerate(small)]

    def acols(d):
        return pl.ds(pl.multiple_of(up(z, NZ, d) * KD, KD), KD)

    def b_load(h):
        return pltpu.make_async_copy(b_hbm.at[:, c, pl.ds(h * SUB, SUB)], b_own.at[h], bl.at[h])

    def b_swap(h):
        return remote(b_hbm.at[:, 1 - c, pl.ds(h * SUB, SUB)], b_sib.at[h], bs.at[h], br.at[h], sibling)

    a_loc = pltpu.make_async_copy(a_hbm.at[:, acols(0)], a_own.at[0], loc_sem)
    a_swap = remote(a_hbm.at[:, acols(0)], a_sib.at[0], fs.at[0], fr.at[0], sibling)
    drive_copy = pltpu.make_async_copy(drive_hbm, drive, drive_sem)
    for copy in small:
        copy.start()
    b_load(0).start()
    a_loc.start()
    pl.semaphore_wait(barrier, len(peers))
    b_swap(0).start()
    a_swap.start()

    def a_send(k):
        d = NZ - ORDER[k]
        return remote(a_hbm.at[:, acols(d)], a_own.at[k], as_.at[k], ar.at[k], zdev(d))

    def leg1(h):
        rows = pl.ds(h * (ROWS // 2), ROWS // 2)
        return remote(a_hbm.at[rows, acols(4)], relay.at[h], hs.at[h], hr.at[h], zdev((2, 6)[h]))

    def leg2(h):
        rows = pl.ds(h * (ROWS // 2), ROWS // 2)
        return remote(relay.at[h], a_own.at[FAR, rows], hs.at[2 + h], hr.at[2 + h], zdev((2, 6)[h]))

    def forward(k):
        return remote(a_own.at[k], a_sib.at[k], fs.at[k], fr.at[k], sibling)

    for k in FIRST:
        a_send(k).start()
    for h in range(1, PER):
        b_swap(h).start()
        b_load(h).start()
    drive_copy.start()
    small[0].wait()

    def looked_up(table, index, width):
        entry = lax.broadcasted_iota(jnp.int32, (table.shape[1], width), 0)
        hits = jnp.where(entry == index[...], 1.0, 0.0).astype(jnp.bfloat16)
        row = jnp.broadcast_to(table[...], (8, table.shape[1]))
        hi = row.astype(jnp.bfloat16).astype(jnp.float32)
        mid = (row - hi).astype(jnp.bfloat16).astype(jnp.float32)
        term = lax.broadcasted_iota(jnp.int32, row.shape, 0)
        terms = jnp.where(term == 0, hi, jnp.where(term == 1, mid, row - hi - mid)).astype(jnp.bfloat16)
        got = lax.dot_general(terms, hits, (((1,), (0,)), ((), ())), preferred_element_type=jnp.float32)
        return got[0:1] + (got[1:2] + got[2:3])

    def energies():
        for copy in small[1:]:
            copy.wait()
        occupied = looked_up(occ, pf, ROWS) + looked_up(occ, ps, ROWS)
        rows = jnp.broadcast_to(occupied, (COLS, ROWS)).T
        first, second = looked_up(virt, af, COLS), looked_up(virt, asec, COLS)
        denominator[...] = (rows - first) - second

    energies()

    limit = sizes[s // 4]
    column = lax.broadcasted_iota(jnp.int32, (SUB, KD), 1)

    def convert(src, h, first, slab_at):
        live = column < limit - (slab_at % 4) * (NZ * KD) - z * KD

        def one(j, carry):
            hi, lo = split(jnp.where(live, src[h, j], 0.0))
            rows = pl.ds(pl.multiple_of(j * SUB, SUB), SUB)
            b3[h, rows, pl.ds(first, KD)] = hi
            b3[h, rows, pl.ds(2 * KD + first, KD)] = lo
            b3[h, rows, pl.ds(4 * KD + first, KD)] = hi
            return carry

        lax.fori_loop(0, NX * NX, one, 0)

    def send1(i):
        p = lax.rem(i, RING)
        src = (
            part.at[p, 0, xo, :, pl.ds(0, QUART)],
            part.at[p, 0, xo, :, pl.ds(QUART, QUART)],
            part.at[p, 1, :, yo, pl.ds(0, QUART)],
            part.at[p, 1, :, yo, pl.ds(QUART, QUART)],
        )
        return [remote(src[k], r1.at[p, k], s1.at[p, k], q1.at[p, k], side[k]) for k in range(4)]

    def send2(i):
        p = lax.rem(i, RING)
        src = (part.at[p, 0, xp], part.at[p, 0, xm], part.at[p, 1, :, yp], part.at[p, 1, :, ym])
        return [remote(src[k], r2.at[p, k], s2.at[p, k], q2.at[p, k], side[k]) for k in range(4)]

    def send3(i):
        p = lax.rem(i, RING)
        src = (
            quad.at[p, 1, xo, pl.ds(0, QUART)],
            quad.at[p, 1, xo, pl.ds(QUART, QUART)],
            quad.at[p, 0, yo, pl.ds(0, QUART)],
            quad.at[p, 0, yo, pl.ds(QUART, QUART)],
        )
        return [remote(src[k], r3.at[p, k], s3.at[p, k], q3.at[p, k], side[k]) for k in range(4)]

    def send4(i):
        p = lax.rem(i, RING)
        src = (quad.at[p, 1, xp], quad.at[p, 1, xm], quad.at[p, 0, yp], quad.at[p, 0, ym])
        return [remote(src[k], r4.at[p, k], s4.at[p, k], q4.at[p, k], side[k]) for k in range(4)]

    def zparts(k):
        return range(2 if k == FAR else 1)

    def zsend(k, h, part_at):
        d, i = ORDER[k], k * PER + h
        if d == 4:
            src, dst, dev = done.at[i, pl.ds(part_at * QUART, QUART)], mh.at[part_at, h], zdev(3 + 2 * part_at)
        elif d < 4:
            src, dst, dev = done.at[i], mg.at[0, d - 2, h], zdev(d - 1)
        else:
            src, dst, dev = done.at[i], mg.at[1, 6 - d, h], zdev(d + 1)
        return remote(src, dst, zs.at[k, h, part_at], zq.at[k, h, part_at], dev)

    def zstart(i):
        for k, d in enumerate(ORDER):
            if d not in (0, 1, 7):
                @pl.when(i // PER == k)
                def _():
                    for n in zparts(k):
                        zsend(k, lax.rem(i, PER), n).start()

    def last(n, h):
        i = ORDER.index((1, 7)[n]) * PER + h
        return remote(done.at[i], fin.at[n, h], es.at[n, h], eq.at[n, h], zdev((1, 7)[n]))

    def merge(n, h):
        for d in ((2, 3), (6, 5))[n]:
            zsend(ORDER.index(d), h, 0).wait_recv()
        zsend(FAR, h, n).wait_recv()
        i = ORDER.index((1, 7)[n]) * PER + h
        done[i] += mg[n, 0, h] + mg[n, 1, h]
        done[i, pl.ds(n * QUART, QUART)] += mh[n, h]
        last(n, h).start()

    def ready(n, h):
        return max(ORDER.index((1, 7)[n]), FAR) * PER + h + 5 <= Z_END

    def stage1(i):
        p = lax.rem(i, RING)
        k = i // PER
        h = lax.rem(i, PER)

        for step_at in range(PER):
            @pl.when(i == step_at)
            def _():
                b_load(step_at).wait()
                convert(b_own, step_at, 0, s)
                if step_at == 0:
                    a_loc.wait()
                b_swap(step_at).wait()
                convert(b_sib, step_at, KD, slab(x, y, 1 - c))

        @pl.when(h == 0)
        def _():
            forward(k).wait_recv()
            for first, source in ((0, a_own), (KD, a_sib)):
                hi, lo = split(source[k])
                a3[:, pl.ds(first, KD)] = hi
                a3[:, pl.ds(2 * KD + first, KD)] = hi
                a3[:, pl.ds(4 * KD + first, KD)] = lo

        def columns(m, carry):
            rows = pl.ds(pl.multiple_of(m * MROWS, MROWS), MROWS)
            acc = lax.dot_general(b3[h, rows, :], a3[...], NT, preferred_element_type=jnp.float32)
            for xx in range(2):
                for yy in range(NX):
                    at = (xx * NX + yy) * SUB
                    for half in range(2):
                        part[p, half, 2 * m + xx, yy] = acc[at:at + SUB, half * LANES:(half + 1) * LANES]
            return carry

        lax.fori_loop(0, NX // 2, columns, 0)
        for copy in send1(i):
            copy.start()

        for begin, blocks in A_BEGIN:
            @pl.when(i == begin)
            def _():
                for kk in blocks:
                    a_send(kk).start()

        @pl.when(i == LEG1_BEGIN)
        def _():
            for half in range(2):
                leg1(half).start()

    def fetch(i):
        k = i // PER

        @pl.when(k + 1 != FAR)
        def _():
            a_wait = remote(a_own.at[k + 1], a_own.at[k + 1], as_.at[k + 1], ar.at[k + 1], sibling)
            a_wait.wait_recv()

        @pl.when(k + 1 == FAR)
        def _():
            for half in range(2):
                leg2(half).wait_recv()

        forward(k + 1).start()

    def stage2(i):
        p = lax.rem(i, RING)
        for copy in send1(i):
            copy.wait()
        part[p, 0, xp, :, pl.ds(0, QUART)] += r1[p, 0]
        part[p, 0, xm, :, pl.ds(QUART, QUART)] += r1[p, 1]
        part[p, 1, :, yp, pl.ds(0, QUART)] += r1[p, 2]
        part[p, 1, :, ym, pl.ds(QUART, QUART)] += r1[p, 3]
        for copy in send2(i):
            copy.start()

    def stage3(i):
        p = lax.rem(i, RING)
        for copy in send2(i):
            copy.wait()
        quad[p, 0] = part[p, 0, x] + (r2[p, 0] + r2[p, 1])
        quad[p, 1] = part[p, 1, :, y] + (r2[p, 2] + r2[p, 3])
        for copy in send3(i):
            copy.start()

    def stage4(i):
        p = lax.rem(i, RING)
        for copy in send3(i):
            copy.wait()
        quad[p, 1, xp, pl.ds(0, QUART)] += r3[p, 0]
        quad[p, 1, xm, pl.ds(QUART, QUART)] += r3[p, 1]
        quad[p, 0, yp, pl.ds(0, QUART)] += r3[p, 2]
        quad[p, 0, ym, pl.ds(QUART, QUART)] += r3[p, 3]
        for copy in send4(i):
            copy.start()

    def stage5(i):
        p = lax.rem(i, RING)
        for copy in send4(i):
            copy.wait()
        done[i, :, pl.ds(0, LANES)] = quad[p, 0, y] + (r4[p, 2] + r4[p, 3])
        done[i, :, pl.ds(LANES, LANES)] = quad[p, 1, x] + (r4[p, 0] + r4[p, 1])

        @pl.when(i > Z_BEGIN - 4)
        def _():
            zstart(i)

    def step(i, carry):
        pl.when(jnp.logical_and(lax.rem(i, PER) == PER - 1, i < STEPS - PER))(functools.partial(fetch, i))
        for lag, stage in enumerate((stage1, stage2, stage3, stage4, stage5)):
            pl.when(jnp.logical_and(i >= lag, i < STEPS + lag))(functools.partial(stage, i - lag))

        @pl.when(i == LEG2_BEGIN)
        def _():
            for half in range(2):
                leg1(half).wait_recv()
                leg2(half).start()

        @pl.when(i == Z_BEGIN)
        def _():
            def begin(j, carry):
                zstart(j)
                return carry

            lax.fori_loop(PER, Z_BEGIN - 3, begin, 0)

        @pl.when(i == Z_END)
        def _():
            for n in range(2):
                for h in range(PER):
                    if ready(n, h):
                        merge(n, h)

        return carry

    lax.fori_loop(0, STEPS + 4, step, 0)

    for n in range(2):
        for h in range(PER):
            if not ready(n, h):
                merge(n, h)
    drive_copy.wait()
    for h in range(PER):
        for n in range(2):
            last(n, h).wait_recv()
        cols = pl.ds(h * SUB, SUB)
        ladder = (done[h] + (fin[0, h] + fin[1, h])).T
        out[:, cols] = (drive[:, cols] + ladder) / denominator[:, cols]
    for n in range(2):
        for h in range(PER):
            last(n, h).wait_send()
    for k, d in enumerate(ORDER):
        if d not in (0, 1, 7):
            for h in range(PER):
                for n in zparts(k):
                    zsend(k, h, n).wait_send()
    a_swap.wait_send()
    for k in range(1, NZ):
        forward(k).wait_send()
    for k in range(1, NZ):
        if k != FAR:
            a_send(k).wait_send()
    for half in range(2):
        leg1(half).wait_send()
        leg2(half).wait_send()


def update(amplitudes, integrals, driver, block_sizes, *tables):
    f32, bf16 = jnp.float32, jnp.bfloat16
    dma = pltpu.SemaphoreType.DMA
    scratch = [
        pltpu.VMEM((ROWS, COLS), f32), dma, pltpu.VMEM((ROWS, COLS), f32),
        pltpu.SMEM((NZ,), jnp.int32),
        *(pltpu.VMEM(table.shape, table.dtype) for table in tables),
        dma((len(tables) + 1,)),
        pltpu.VMEM((NZ, ROWS, KD), f32),
        pltpu.VMEM((NZ, ROWS, KD), f32),
        pltpu.VMEM((2, ROWS // 2, KD), f32),
        pltpu.VMEM((PER, NX * NX, SUB, KD), f32),
        pltpu.VMEM((PER, NX * NX, SUB, KD), f32),
        pltpu.VMEM((ROWS, 6 * KD), bf16),
        pltpu.VMEM((PER, NX * NX * SUB, 6 * KD), bf16),
        pltpu.VMEM((RING, 2, NX, NX, SUB, LANES), f32),
        pltpu.VMEM((RING, 2, NX, SUB, LANES), f32),
        pltpu.VMEM((STEPS, SUB, ROWS), f32),
        pltpu.VMEM((RING, 4, NX, QUART, LANES), f32),
        pltpu.VMEM((RING, 4, NX, SUB, LANES), f32),
        pltpu.VMEM((RING, 4, QUART, LANES), f32),
        pltpu.VMEM((RING, 4, SUB, LANES), f32),
        pltpu.VMEM((2, 2, PER, SUB, ROWS), f32),
        pltpu.VMEM((2, PER, QUART, ROWS), f32),
        pltpu.VMEM((2, PER, SUB, ROWS), f32),
        dma, dma((PER,)), dma((PER,)), dma((PER,)),
        dma((NZ,)), dma((NZ,)), dma((4,)), dma((4,)), dma((NZ,)), dma((NZ,)),
        dma((RING, 4)), dma((RING, 4)), dma((RING, 4)), dma((RING, 4)),
        dma((RING, 4)), dma((RING, 4)), dma((RING, 4)), dma((RING, 4)),
        dma((NZ, PER, 2)), dma((NZ, PER, 2)), dma((2, PER)), dma((2, PER)),
    ]
    return pl.pallas_call(
        ladder_kernel,
        out_shape=jax.ShapeDtypeStruct((ROWS, COLS), f32),
        in_specs=[pl.BlockSpec(memory_space=pltpu.HBM)] * (4 + len(tables)),
        out_specs=pl.BlockSpec(memory_space=pltpu.VMEM),
        scratch_shapes=scratch,
        compiler_params=pltpu.CompilerParams(
            collective_id=0, has_side_effects=True, vmem_limit_bytes=60 * 1024 * 1024
        ),
        cost_estimate=pl.CostEstimate(
            flops=3 * 2 * 2048 * 2048 * 768, bytes_accessed=12 * 1024 * 1024, transcendentals=0
        ),
        name="ladder",
    )(block_sizes, amplitudes, integrals.reshape(NX * NX, 2, COLS, KD), *tables, driver)


def body(
    amplitudes,
    integrals,
    driver,
    block_sizes,
    pair_first,
    pair_second,
    ab_first,
    ab_second,
    occ_energy,
    virt_energy,
):
    tables = (pair_first, pair_second, ab_first, ab_second, occ_energy, virt_energy)
    return update(amplitudes, integrals, driver, block_sizes, *(table[None] for table in tables))


def solution(mesh):
    placed = (
        P("pair", "slab"),
        P(None, ("slab", "pair")),
        P("pair", "slab"),
        P(),
        P("pair"),
        P("pair"),
        P("slab"),
        P("slab"),
        P(),
        P(),
    )
    return jax.shard_map(
        body, mesh=mesh, in_specs=placed, out_specs=P("pair", "slab"), check_vma=False
    )
```

```python
import functools

import jax
import jax.numpy as jnp
from jax import lax
from jax.experimental import pallas as pl
from jax.experimental.pallas import tpu as pltpu
from jax.sharding import PartitionSpec as P

MESH = pl.DeviceIdType.MESH
NT = (((1,), (1,)), ((), ()))

NZ = 8
NX = 4
ROWS = 256
KD = 384
COLS = 128
SUB = 64
PER = COLS // SUB
QUART = SUB // 2
STEPS = NZ * PER
LANES = 128
MROWS = 2 * NX * SUB
RING = 4
ORDER = (0, 1, 7, 2, 6, 3, 5, 4)
FAR = ORDER.index(4)
TABLE = [(0, h) for h in range(PER // 2)] + [(k, h) for k in range(1, NZ) for h in range(PER)]
TABLE += [(0, h) for h in range(PER // 2, PER)]
AT = {entry: i for i, entry in enumerate(TABLE)}
PART_AT = [min(i for i, entry in enumerate(TABLE) if entry[1] == h) for h in range(PER)]
BLOCK_AT = [i for i, entry in enumerate(TABLE) if i == 0 or TABLE[i - 1][0] != entry[0]]
FETCH_AT = [AT[k, 0] - 1 for k in range(NZ)]
FIRST = (1, 2)
A_BEGIN = ((0, (3, 4)), (2, (5, 6)))
LEG1_BEGIN = 4
LEG2_BEGIN = 9
Z_BEGIN = 12
Z_END = STEPS + 2


def split(v):
    hi = v.astype(jnp.bfloat16)
    lo = (v - hi.astype(jnp.float32)).astype(jnp.bfloat16)
    return hi, lo


def ladder_kernel(
    sizes_hbm, a_hbm, b_hbm, pf_hbm, ps_hbm, af_hbm, as_hbm, occ_hbm, virt_hbm, drive_hbm, out,
    drive, drive_sem, denominator, sizes, pf, ps, af, asec, occ, virt, small_sem, a_own, a_sib, relay, b_own, b_sib, a3, b3, part, quad, done,
    r1, r2, r3, r4, mg, mh, fin,
    loc_sem, bl, bs, br, as_, ar, hs, hr, fs, fr, s1, q1, s2, q2, s3, q3, s4, q4, zs, zq, es, eq,
):
    z = lax.axis_index("pair")
    s = lax.axis_index("slab")
    x, y, c = s // (2 * NX), (s // 2) % NX, s % 2

    def slab(xx, yy, cc):
        return (xx * NX + yy) * 2 + cc

    def up(v, n, d):
        return lax.rem(v + d, n)

    xp, xo, xm = up(x, NX, 1), up(x, NX, 2), up(x, NX, 3)
    yp, yo, ym = up(y, NX, 1), up(y, NX, 2), up(y, NX, 3)
    sibling = (z, slab(x, y, 1 - c))
    side = ((z, slab(xp, y, c)), (z, slab(xm, y, c)), (z, slab(x, yp, c)), (z, slab(x, ym, c)))

    def zdev(d):
        return (up(z, NZ, d), s)

    def remote(src, dst, send, recv, dev):
        return pltpu.make_async_remote_copy(
            src_ref=src, dst_ref=dst, send_sem=send, recv_sem=recv, device_id=dev, device_id_type=MESH
        )

    barrier = pltpu.get_barrier_semaphore()
    peers = [sibling, *side] + [zdev(d) for d in range(1, NZ)]
    for dev in peers:
        pl.semaphore_signal(barrier, inc=1, device_id=dev, device_id_type=MESH)

    small = ((sizes_hbm, sizes), (pf_hbm, pf), (ps_hbm, ps), (af_hbm, af), (as_hbm, asec), (occ_hbm, occ), (virt_hbm, virt))
    small = [pltpu.make_async_copy(src, dst, small_sem.at[n]) for n, (src, dst) in enumerate(small)]

    def acols(d):
        return pl.ds(pl.multiple_of(up(z, NZ, d) * KD, KD), KD)

    def b_load(h):
        return pltpu.make_async_copy(b_hbm.at[:, c, pl.ds(h * SUB, SUB)], b_own.at[h], bl.at[h])

    def b_swap(h):
        return remote(b_hbm.at[:, 1 - c, pl.ds(h * SUB, SUB)], b_sib.at[h], bs.at[h], br.at[h], sibling)

    a_loc = pltpu.make_async_copy(a_hbm.at[:, acols(0)], a_own.at[0], loc_sem)
    a_swap = remote(a_hbm.at[:, acols(0)], a_sib.at[0], fs.at[0], fr.at[0], sibling)
    drive_copy = pltpu.make_async_copy(drive_hbm, drive, drive_sem)
    for copy in small:
        copy.start()
    b_load(0).start()
    a_loc.start()
    pl.semaphore_wait(barrier, len(peers))
    b_swap(0).start()
    a_swap.start()

    def a_send(k):
        d = NZ - ORDER[k]
        return remote(a_hbm.at[:, acols(d)], a_own.at[k], as_.at[k], ar.at[k], zdev(d))

    def leg1(h):
        rows = pl.ds(h * (ROWS // 2), ROWS // 2)
        return remote(a_hbm.at[rows, acols(4)], relay.at[h], hs.at[h], hr.at[h], zdev((2, 6)[h]))

    def leg2(h):
        rows = pl.ds(h * (ROWS // 2), ROWS // 2)
        return remote(relay.at[h], a_own.at[FAR, rows], hs.at[2 + h], hr.at[2 + h], zdev((2, 6)[h]))

    def forward(k):
        return remote(a_own.at[k], a_sib.at[k], fs.at[k], fr.at[k], sibling)

    for k in FIRST:
        a_send(k).start()
    for h in range(1, PER):
        b_swap(h).start()
        b_load(h).start()
    drive_copy.start()
    small[0].wait()

    def looked_up(table, index, width):
        entry = lax.broadcasted_iota(jnp.int32, (table.shape[1], width), 0)
        hits = jnp.where(entry == index[...], 1.0, 0.0).astype(jnp.bfloat16)
        row = jnp.broadcast_to(table[...], (8, table.shape[1]))
        hi = row.astype(jnp.bfloat16).astype(jnp.float32)
        mid = (row - hi).astype(jnp.bfloat16).astype(jnp.float32)
        term = lax.broadcasted_iota(jnp.int32, row.shape, 0)
        terms = jnp.where(term == 0, hi, jnp.where(term == 1, mid, row - hi - mid)).astype(jnp.bfloat16)
        got = lax.dot_general(terms, hits, (((1,), (0,)), ((), ())), preferred_element_type=jnp.float32)
        return got[0:1] + (got[1:2] + got[2:3])

    def energies():
        for copy in small[1:]:
            copy.wait()
        occupied = looked_up(occ, pf, ROWS) + looked_up(occ, ps, ROWS)
        rows = jnp.broadcast_to(occupied, (COLS, ROWS)).T
        first, second = looked_up(virt, af, COLS), looked_up(virt, asec, COLS)
        denominator[...] = (rows - first) - second

    energies()

    limit = sizes[s // 4]
    column = lax.broadcasted_iota(jnp.int32, (SUB, KD), 1)

    def convert(src, h, first, slab_at):
        live = column < limit - (slab_at % 4) * (NZ * KD) - z * KD

        def one(j, carry):
            hi, lo = split(jnp.where(live, src[h, j], 0.0))
            rows = pl.ds(pl.multiple_of(j * SUB, SUB), SUB)
            b3[h, rows, pl.ds(first, KD)] = hi
            b3[h, rows, pl.ds(2 * KD + first, KD)] = lo
            b3[h, rows, pl.ds(4 * KD + first, KD)] = hi
            return carry

        lax.fori_loop(0, NX * NX, one, 0)

    def send1(i):
        p = lax.rem(i, RING)
        src = (
            part.at[p, 0, xo, :, pl.ds(0, QUART)],
            part.at[p, 0, xo, :, pl.ds(QUART, QUART)],
            part.at[p, 1, :, yo, pl.ds(0, QUART)],
            part.at[p, 1, :, yo, pl.ds(QUART, QUART)],
        )
        return [remote(src[k], r1.at[p, k], s1.at[p, k], q1.at[p, k], side[k]) for k in range(4)]

    def send2(i):
        p = lax.rem(i, RING)
        src = (part.at[p, 0, xp], part.at[p, 0, xm], part.at[p, 1, :, yp], part.at[p, 1, :, ym])
        return [remote(src[k], r2.at[p, k], s2.at[p, k], q2.at[p, k], side[k]) for k in range(4)]

    def send3(i):
        p = lax.rem(i, RING)
        src = (
            quad.at[p, 1, xo, pl.ds(0, QUART)],
            quad.at[p, 1, xo, pl.ds(QUART, QUART)],
            quad.at[p, 0, yo, pl.ds(0, QUART)],
            quad.at[p, 0, yo, pl.ds(QUART, QUART)],
        )
        return [remote(src[k], r3.at[p, k], s3.at[p, k], q3.at[p, k], side[k]) for k in range(4)]

    def send4(i):
        p = lax.rem(i, RING)
        src = (quad.at[p, 1, xp], quad.at[p, 1, xm], quad.at[p, 0, yp], quad.at[p, 0, ym])
        return [remote(src[k], r4.at[p, k], s4.at[p, k], q4.at[p, k], side[k]) for k in range(4)]

    def zparts(k):
        return range(2 if k == FAR else 1)

    def zsend(i, k, h, part_at):
        d = ORDER[k]
        if d == 4:
            src, dst, dev = done.at[i, pl.ds(part_at * QUART, QUART)], mh.at[part_at, h], zdev(3 + 2 * part_at)
        elif d < 4:
            src, dst, dev = done.at[i], mg.at[0, d - 2, h], zdev(d - 1)
        else:
            src, dst, dev = done.at[i], mg.at[1, 6 - d, h], zdev(d + 1)
        return remote(src, dst, zs.at[k, h, part_at], zq.at[k, h, part_at], dev)

    def entry(i):
        k = sum(jnp.where(i == at, block, 0) for at, (block, h) in enumerate(TABLE))
        return k, sum(jnp.where(i == at, h, 0) for at, (block, h) in enumerate(TABLE))

    def zstart(i):
        block, h = entry(i)
        for k, d in enumerate(ORDER):
            if d not in (0, 1, 7):
                @pl.when(block == k)
                def _():
                    for n in zparts(k):
                        zsend(i, k, h, n).start()

    def last(n, h):
        i = AT[ORDER.index((1, 7)[n]), h]
        return remote(done.at[i], fin.at[n, h], es.at[n, h], eq.at[n, h], zdev((1, 7)[n]))

    def merge(n, h):
        for d in ((2, 3), (6, 5))[n]:
            k = ORDER.index(d)
            zsend(AT[k, h], k, h, 0).wait_recv()
        zsend(AT[FAR, h], FAR, h, n).wait_recv()
        i = AT[ORDER.index((1, 7)[n]), h]
        done[i] += mg[n, 0, h] + mg[n, 1, h]
        done[i, pl.ds(n * QUART, QUART)] += mh[n, h]
        last(n, h).start()

    def ready(n, h):
        return max(AT[ORDER.index((1, 7)[n]), h], AT[FAR, h]) + 5 <= Z_END

    def stage1(i):
        p = lax.rem(i, RING)
        k, h = entry(i)

        for step_at in range(PER):
            @pl.when(i == PART_AT[step_at])
            def _():
                b_load(step_at).wait()
                convert(b_own, step_at, 0, s)
                if step_at == 0:
                    a_loc.wait()
                b_swap(step_at).wait()
                convert(b_sib, step_at, KD, slab(x, y, 1 - c))

        @pl.when(functools.reduce(jnp.logical_or, [i == at for at in BLOCK_AT[:-1]]))
        def _():
            forward(k).wait_recv()

        @pl.when(functools.reduce(jnp.logical_or, [i == at for at in BLOCK_AT]))
        def _():
            for first, source in ((0, a_own), (KD, a_sib)):
                hi, lo = split(source[k])
                a3[:, pl.ds(first, KD)] = hi
                a3[:, pl.ds(2 * KD + first, KD)] = hi
                a3[:, pl.ds(4 * KD + first, KD)] = lo

        def columns(m, carry):
            rows = pl.ds(pl.multiple_of(m * MROWS, MROWS), MROWS)
            acc = lax.dot_general(b3[h, rows, :], a3[...], NT, preferred_element_type=jnp.float32)
            for xx in range(2):
                for yy in range(NX):
                    at = (xx * NX + yy) * SUB
                    for half in range(2):
                        part[p, half, 2 * m + xx, yy] = acc[at:at + SUB, half * LANES:(half + 1) * LANES]
            return carry

        lax.fori_loop(0, NX // 2, columns, 0)
        for copy in send1(i):
            copy.start()

        for begin, blocks in A_BEGIN:
            @pl.when(i == begin)
            def _():
                for kk in blocks:
                    a_send(kk).start()

        @pl.when(i == LEG1_BEGIN)
        def _():
            for half in range(2):
                leg1(half).start()

    def fetch(k):
        if k == FAR:
            for half in range(2):
                leg2(half).wait_recv()
        else:
            a_send(k).wait_recv()
        forward(k).start()

    def stage2(i):
        p = lax.rem(i, RING)
        for copy in send1(i):
            copy.wait()
        part[p, 0, xp, :, pl.ds(0, QUART)] += r1[p, 0]
        part[p, 0, xm, :, pl.ds(QUART, QUART)] += r1[p, 1]
        part[p, 1, :, yp, pl.ds(0, QUART)] += r1[p, 2]
        part[p, 1, :, ym, pl.ds(QUART, QUART)] += r1[p, 3]
        for copy in send2(i):
            copy.start()

    def stage3(i):
        p = lax.rem(i, RING)
        for copy in send2(i):
            copy.wait()
        quad[p, 0] = part[p, 0, x] + (r2[p, 0] + r2[p, 1])
        quad[p, 1] = part[p, 1, :, y] + (r2[p, 2] + r2[p, 3])
        for copy in send3(i):
            copy.start()

    def stage4(i):
        p = lax.rem(i, RING)
        for copy in send3(i):
            copy.wait()
        quad[p, 1, xp, pl.ds(0, QUART)] += r3[p, 0]
        quad[p, 1, xm, pl.ds(QUART, QUART)] += r3[p, 1]
        quad[p, 0, yp, pl.ds(0, QUART)] += r3[p, 2]
        quad[p, 0, ym, pl.ds(QUART, QUART)] += r3[p, 3]
        for copy in send4(i):
            copy.start()

    def stage5(i):
        p = lax.rem(i, RING)
        for copy in send4(i):
            copy.wait()
        done[i, :, pl.ds(0, LANES)] = quad[p, 0, y] + (r4[p, 2] + r4[p, 3])
        done[i, :, pl.ds(LANES, LANES)] = quad[p, 1, x] + (r4[p, 0] + r4[p, 1])

        @pl.when(i > Z_BEGIN - 4)
        def _():
            zstart(i)

    def step(i, carry):
        for k in range(2, NZ):
            pl.when(i == FETCH_AT[k])(functools.partial(fetch, k))
        for lag, stage in enumerate((stage1, stage2, stage3, stage4, stage5)):
            pl.when(jnp.logical_and(i >= lag, i < STEPS + lag))(functools.partial(stage, i - lag))
            if lag == 0:
                pl.when(i == FETCH_AT[1])(functools.partial(fetch, 1))

        @pl.when(i == LEG2_BEGIN)
        def _():
            for half in range(2):
                leg1(half).wait_recv()
                leg2(half).start()

        @pl.when(i == Z_BEGIN)
        def _():
            def begin(j, carry):
                zstart(j)
                return carry

            lax.fori_loop(0, Z_BEGIN - 3, begin, 0)

        @pl.when(i == Z_END)
        def _():
            for n in range(2):
                for h in range(PER):
                    if ready(n, h):
                        merge(n, h)

        return carry

    lax.fori_loop(0, STEPS + 4, step, 0)

    for n in range(2):
        for h in range(PER):
            if not ready(n, h):
                merge(n, h)
    drive_copy.wait()
    for h in range(PER):
        for n in range(2):
            last(n, h).wait_recv()
        cols = pl.ds(h * SUB, SUB)
        ladder = (done[AT[0, h]] + (fin[0, h] + fin[1, h])).T
        out[:, cols] = (drive[:, cols] + ladder) / denominator[:, cols]
    for n in range(2):
        for h in range(PER):
            last(n, h).wait_send()
    for k, d in enumerate(ORDER):
        if d not in (0, 1, 7):
            for h in range(PER):
                for n in zparts(k):
                    zsend(AT[k, h], k, h, n).wait_send()
    a_swap.wait_send()
    for k in range(1, NZ):
        forward(k).wait_send()
    for k in range(1, NZ):
        if k != FAR:
            a_send(k).wait_send()
    for half in range(2):
        leg1(half).wait_send()
        leg2(half).wait_send()


def update(amplitudes, integrals, driver, block_sizes, *tables):
    f32, bf16 = jnp.float32, jnp.bfloat16
    dma = pltpu.SemaphoreType.DMA
    scratch = [
        pltpu.VMEM((ROWS, COLS), f32), dma, pltpu.VMEM((ROWS, COLS), f32),
        pltpu.SMEM((NZ,), jnp.int32),
        *(pltpu.VMEM(table.shape, table.dtype) for table in tables),
        dma((len(tables) + 1,)),
        pltpu.VMEM((NZ, ROWS, KD), f32),
        pltpu.VMEM((NZ, ROWS, KD), f32),
        pltpu.VMEM((2, ROWS // 2, KD), f32),
        pltpu.VMEM((PER, NX * NX, SUB, KD), f32),
        pltpu.VMEM((PER, NX * NX, SUB, KD), f32),
        pltpu.VMEM((ROWS, 6 * KD), bf16),
        pltpu.VMEM((PER, NX * NX * SUB, 6 * KD), bf16),
        pltpu.VMEM((RING, 2, NX, NX, SUB, LANES), f32),
        pltpu.VMEM((RING, 2, NX, SUB, LANES), f32),
        pltpu.VMEM((STEPS, SUB, ROWS), f32),
        pltpu.VMEM((RING, 4, NX, QUART, LANES), f32),
        pltpu.VMEM((RING, 4, NX, SUB, LANES), f32),
        pltpu.VMEM((RING, 4, QUART, LANES), f32),
        pltpu.VMEM((RING, 4, SUB, LANES), f32),
        pltpu.VMEM((2, 2, PER, SUB, ROWS), f32),
        pltpu.VMEM((2, PER, QUART, ROWS), f32),
        pltpu.VMEM((2, PER, SUB, ROWS), f32),
        dma, dma((PER,)), dma((PER,)), dma((PER,)),
        dma((NZ,)), dma((NZ,)), dma((4,)), dma((4,)), dma((NZ,)), dma((NZ,)),
        dma((RING, 4)), dma((RING, 4)), dma((RING, 4)), dma((RING, 4)),
        dma((RING, 4)), dma((RING, 4)), dma((RING, 4)), dma((RING, 4)),
        dma((NZ, PER, 2)), dma((NZ, PER, 2)), dma((2, PER)), dma((2, PER)),
    ]
    return pl.pallas_call(
        ladder_kernel,
        out_shape=jax.ShapeDtypeStruct((ROWS, COLS), f32),
        in_specs=[pl.BlockSpec(memory_space=pltpu.HBM)] * (4 + len(tables)),
        out_specs=pl.BlockSpec(memory_space=pltpu.VMEM),
        scratch_shapes=scratch,
        compiler_params=pltpu.CompilerParams(
            collective_id=0, has_side_effects=True, vmem_limit_bytes=60 * 1024 * 1024
        ),
        cost_estimate=pl.CostEstimate(
            flops=3 * 2 * 2048 * 2048 * 768, bytes_accessed=12 * 1024 * 1024, transcendentals=0
        ),
        name="ladder",
    )(block_sizes, amplitudes, integrals.reshape(NX * NX, 2, COLS, KD), *tables, driver)


def body(
    amplitudes,
    integrals,
    driver,
    block_sizes,
    pair_first,
    pair_second,
    ab_first,
    ab_second,
    occ_energy,
    virt_energy,
):
    tables = (pair_first, pair_second, ab_first, ab_second, occ_energy, virt_energy)
    return update(amplitudes, integrals, driver, block_sizes, *(table[None] for table in tables))


def solution(mesh):
    placed = (
        P("pair", "slab"),
        P(None, ("slab", "pair")),
        P("pair", "slab"),
        P(),
        P("pair"),
        P("pair"),
        P("slab"),
        P("slab"),
        P(),
        P(),
    )
    return jax.shard_map(
        body, mesh=mesh, in_specs=placed, out_specs=P("pair", "slab"), check_vma=False
    )
```

```python
import functools

import jax
import jax.numpy as jnp
from jax import lax
from jax.experimental import pallas as pl
from jax.experimental.pallas import tpu as pltpu
from jax.sharding import PartitionSpec as P

MESH = pl.DeviceIdType.MESH
NT = (((1,), (1,)), ((), ()))

NZ = 8
NX = 4
ROWS = 256
KD = 384
COLS = 128
SUB = 64
PER = COLS // SUB
QUART = SUB // 2
STEPS = NZ * PER
LANES = 128
MROWS = 2 * NX * SUB
RING = 4
ORDER = (0, 1, 7, 2, 6, 3, 5, 4)
FAR = ORDER.index(4)
TABLE = [(0, h) for h in range(PER // 2)] + [(k, h) for k in range(1, NZ) for h in range(PER)]
TABLE += [(0, h) for h in range(PER // 2, PER)]
AT = {entry: i for i, entry in enumerate(TABLE)}
PART_AT = [min(i for i, entry in enumerate(TABLE) if entry[1] == h) for h in range(PER)]
BLOCK_AT = [i for i, entry in enumerate(TABLE) if i == 0 or TABLE[i - 1][0] != entry[0]]
FETCH_AT = [AT[k, 0] - 1 for k in range(NZ)]
FIRST = (1, 2)
SECOND = (3, 4)
A_BEGIN = ((2, (5, 6)),)
LEG1_BEGIN = 4
LEG2_BEGIN = 9
Z_BEGIN = 12
Z_END = STEPS + 2


def split(v):
    hi = v.astype(jnp.bfloat16)
    lo = (v - hi.astype(jnp.float32)).astype(jnp.bfloat16)
    return hi, lo


def ladder_kernel(
    sizes_hbm, a_hbm, b_hbm, pf_hbm, ps_hbm, af_hbm, as_hbm, occ_hbm, virt_hbm, drive_hbm, out,
    drive, drive_sem, denominator, sizes, pf, ps, af, asec, occ, virt, small_sem, a_own, a_sib, relay, b_own, b_sib, a3, b3, part, quad, done,
    r1, r2, r3, r4, mg, mh, fin,
    loc_sem, bl, bs, br, as_, ar, hs, hr, fs, fr, s1, q1, s2, q2, s3, q3, s4, q4, zs, zq, es, eq,
):
    z = lax.axis_index("pair")
    s = lax.axis_index("slab")
    x, y, c = s // (2 * NX), (s // 2) % NX, s % 2

    def slab(xx, yy, cc):
        return (xx * NX + yy) * 2 + cc

    def up(v, n, d):
        return lax.rem(v + d, n)

    xp, xo, xm = up(x, NX, 1), up(x, NX, 2), up(x, NX, 3)
    yp, yo, ym = up(y, NX, 1), up(y, NX, 2), up(y, NX, 3)
    sibling = (z, slab(x, y, 1 - c))
    side = ((z, slab(xp, y, c)), (z, slab(xm, y, c)), (z, slab(x, yp, c)), (z, slab(x, ym, c)))

    def zdev(d):
        return (up(z, NZ, d), s)

    def remote(src, dst, send, recv, dev):
        return pltpu.make_async_remote_copy(
            src_ref=src, dst_ref=dst, send_sem=send, recv_sem=recv, device_id=dev, device_id_type=MESH
        )

    barrier = pltpu.get_barrier_semaphore()
    peers = [sibling, *side] + [zdev(d) for d in range(1, NZ)]
    for dev in peers:
        pl.semaphore_signal(barrier, inc=1, device_id=dev, device_id_type=MESH)

    small = ((sizes_hbm, sizes), (pf_hbm, pf), (ps_hbm, ps), (af_hbm, af), (as_hbm, asec), (occ_hbm, occ), (virt_hbm, virt))
    small = [pltpu.make_async_copy(src, dst, small_sem.at[n]) for n, (src, dst) in enumerate(small)]

    def acols(d):
        return pl.ds(pl.multiple_of(up(z, NZ, d) * KD, KD), KD)

    def b_load(h):
        return pltpu.make_async_copy(b_hbm.at[:, c, pl.ds(h * SUB, SUB)], b_own.at[h], bl.at[h])

    def b_swap(h):
        return remote(b_hbm.at[:, 1 - c, pl.ds(h * SUB, SUB)], b_sib.at[h], bs.at[h], br.at[h], sibling)

    a_loc = pltpu.make_async_copy(a_hbm.at[:, acols(0)], a_own.at[0], loc_sem)
    a_swap = remote(a_hbm.at[:, acols(0)], a_sib.at[0], fs.at[0], fr.at[0], sibling)
    drive_copy = pltpu.make_async_copy(drive_hbm, drive, drive_sem)
    for copy in small:
        copy.start()
    b_load(0).start()
    a_loc.start()
    pl.semaphore_wait(barrier, len(peers))
    b_swap(0).start()
    a_swap.start()

    def a_send(k):
        d = NZ - ORDER[k]
        return remote(a_hbm.at[:, acols(d)], a_own.at[k], as_.at[k], ar.at[k], zdev(d))

    def leg1(h):
        rows = pl.ds(h * (ROWS // 2), ROWS // 2)
        return remote(a_hbm.at[rows, acols(4)], relay.at[h], hs.at[h], hr.at[h], zdev((2, 6)[h]))

    def leg2(h):
        rows = pl.ds(h * (ROWS // 2), ROWS // 2)
        return remote(relay.at[h], a_own.at[FAR, rows], hs.at[2 + h], hr.at[2 + h], zdev((2, 6)[h]))

    def forward(k):
        return remote(a_own.at[k], a_sib.at[k], fs.at[k], fr.at[k], sibling)

    for k in FIRST:
        a_send(k).start()
    drive_copy.start()
    small[0].wait()

    def looked_up(table, index, width):
        entry = lax.broadcasted_iota(jnp.int32, (table.shape[1], width), 0)
        hits = jnp.where(entry == index[...], 1.0, 0.0).astype(jnp.bfloat16)
        row = jnp.broadcast_to(table[...], (8, table.shape[1]))
        hi = row.astype(jnp.bfloat16).astype(jnp.float32)
        mid = (row - hi).astype(jnp.bfloat16).astype(jnp.float32)
        term = lax.broadcasted_iota(jnp.int32, row.shape, 0)
        terms = jnp.where(term == 0, hi, jnp.where(term == 1, mid, row - hi - mid)).astype(jnp.bfloat16)
        got = lax.dot_general(terms, hits, (((1,), (0,)), ((), ())), preferred_element_type=jnp.float32)
        return got[0:1] + (got[1:2] + got[2:3])

    def energies():
        for copy in small[1:]:
            copy.wait()
        occupied = looked_up(occ, pf, ROWS) + looked_up(occ, ps, ROWS)
        rows = jnp.broadcast_to(occupied, (COLS, ROWS)).T
        first, second = looked_up(virt, af, COLS), looked_up(virt, asec, COLS)
        denominator[...] = (rows - first) - second

    energies()

    limit = sizes[s // 4]
    column = lax.broadcasted_iota(jnp.int32, (SUB, KD), 1)

    def convert(src, h, first, slab_at):
        live = column < limit - (slab_at % 4) * (NZ * KD) - z * KD

        def one(j, carry):
            hi, lo = split(jnp.where(live, src[h, j], 0.0))
            rows = pl.ds(pl.multiple_of(j * SUB, SUB), SUB)
            b3[h, rows, pl.ds(first, KD)] = hi
            b3[h, rows, pl.ds(2 * KD + first, KD)] = lo
            b3[h, rows, pl.ds(4 * KD + first, KD)] = hi
            return carry

        lax.fori_loop(0, NX * NX, one, 0)

    def send1(i):
        p = lax.rem(i, RING)
        src = (
            part.at[p, 0, xo, :, pl.ds(0, QUART)],
            part.at[p, 0, xo, :, pl.ds(QUART, QUART)],
            part.at[p, 1, :, yo, pl.ds(0, QUART)],
            part.at[p, 1, :, yo, pl.ds(QUART, QUART)],
        )
        return [remote(src[k], r1.at[p, k], s1.at[p, k], q1.at[p, k], side[k]) for k in range(4)]

    def send2(i):
        p = lax.rem(i, RING)
        src = (part.at[p, 0, xp], part.at[p, 0, xm], part.at[p, 1, :, yp], part.at[p, 1, :, ym])
        return [remote(src[k], r2.at[p, k], s2.at[p, k], q2.at[p, k], side[k]) for k in range(4)]

    def send3(i):
        p = lax.rem(i, RING)
        src = (
            quad.at[p, 1, xo, pl.ds(0, QUART)],
            quad.at[p, 1, xo, pl.ds(QUART, QUART)],
            quad.at[p, 0, yo, pl.ds(0, QUART)],
            quad.at[p, 0, yo, pl.ds(QUART, QUART)],
        )
        return [remote(src[k], r3.at[p, k], s3.at[p, k], q3.at[p, k], side[k]) for k in range(4)]

    def send4(i):
        p = lax.rem(i, RING)
        src = (quad.at[p, 1, xp], quad.at[p, 1, xm], quad.at[p, 0, yp], quad.at[p, 0, ym])
        return [remote(src[k], r4.at[p, k], s4.at[p, k], q4.at[p, k], side[k]) for k in range(4)]

    def zparts(k):
        return range(2 if k == FAR else 1)

    def zsend(i, k, h, part_at):
        d = ORDER[k]
        if d == 4:
            src, dst, dev = done.at[i, pl.ds(part_at * QUART, QUART)], mh.at[part_at, h], zdev(3 + 2 * part_at)
        elif d < 4:
            src, dst, dev = done.at[i], mg.at[0, d - 2, h], zdev(d - 1)
        else:
            src, dst, dev = done.at[i], mg.at[1, 6 - d, h], zdev(d + 1)
        return remote(src, dst, zs.at[k, h, part_at], zq.at[k, h, part_at], dev)

    def entry(i):
        k = sum(jnp.where(i == at, block, 0) for at, (block, h) in enumerate(TABLE))
        return k, sum(jnp.where(i == at, h, 0) for at, (block, h) in enumerate(TABLE))

    def zstart(i):
        block, h = entry(i)
        for k, d in enumerate(ORDER):
            if d not in (0, 1, 7):
                @pl.when(block == k)
                def _():
                    for n in zparts(k):
                        zsend(i, k, h, n).start()

    def last(n, h):
        i = AT[ORDER.index((1, 7)[n]), h]
        return remote(done.at[i], fin.at[n, h], es.at[n, h], eq.at[n, h], zdev((1, 7)[n]))

    def merge(n, h):
        for d in ((2, 3), (6, 5))[n]:
            k = ORDER.index(d)
            zsend(AT[k, h], k, h, 0).wait_recv()
        zsend(AT[FAR, h], FAR, h, n).wait_recv()
        i = AT[ORDER.index((1, 7)[n]), h]
        done[i] += mg[n, 0, h] + mg[n, 1, h]
        done[i, pl.ds(n * QUART, QUART)] += mh[n, h]
        last(n, h).start()

    def ready(n, h):
        return max(AT[ORDER.index((1, 7)[n]), h], AT[FAR, h]) + 5 <= Z_END

    def stage1(i):
        p = lax.rem(i, RING)
        k, h = entry(i)

        for step_at in range(PER):
            @pl.when(i == PART_AT[step_at])
            def _():
                b_load(step_at).wait()
                convert(b_own, step_at, 0, s)
                if step_at == 0:
                    a_loc.wait()
                    for kk in SECOND:
                        a_send(kk).start()
                b_swap(step_at).wait()
                convert(b_sib, step_at, KD, slab(x, y, 1 - c))
                if step_at + 1 < PER:
                    b_swap(step_at + 1).start()
                    b_load(step_at + 1).start()

        @pl.when(functools.reduce(jnp.logical_or, [i == at for at in BLOCK_AT[:-1]]))
        def _():
            forward(k).wait_recv()

        @pl.when(functools.reduce(jnp.logical_or, [i == at for at in BLOCK_AT]))
        def _():
            for first, source in ((0, a_own), (KD, a_sib)):
                hi, lo = split(source[k])
                a3[:, pl.ds(first, KD)] = hi
                a3[:, pl.ds(2 * KD + first, KD)] = hi
                a3[:, pl.ds(4 * KD + first, KD)] = lo

        def columns(m, carry):
            rows = pl.ds(pl.multiple_of(m * MROWS, MROWS), MROWS)
            acc = lax.dot_general(b3[h, rows, :], a3[...], NT, preferred_element_type=jnp.float32)
            for xx in range(2):
                for yy in range(NX):
                    at = (xx * NX + yy) * SUB
                    for half in range(2):
                        part[p, half, 2 * m + xx, yy] = acc[at:at + SUB, half * LANES:(half + 1) * LANES]
            return carry

        lax.fori_loop(0, NX // 2, columns, 0)
        for copy in send1(i):
            copy.start()

        for begin, blocks in A_BEGIN:
            @pl.when(i == begin)
            def _():
                for kk in blocks:
                    a_send(kk).start()

        @pl.when(i == LEG1_BEGIN)
        def _():
            for half in range(2):
                leg1(half).start()

    def fetch(k):
        if k == FAR:
            for half in range(2):
                leg2(half).wait_recv()
        else:
            a_send(k).wait_recv()
        forward(k).start()

    def stage2(i):
        p = lax.rem(i, RING)
        for copy in send1(i):
            copy.wait()
        part[p, 0, xp, :, pl.ds(0, QUART)] += r1[p, 0]
        part[p, 0, xm, :, pl.ds(QUART, QUART)] += r1[p, 1]
        part[p, 1, :, yp, pl.ds(0, QUART)] += r1[p, 2]
        part[p, 1, :, ym, pl.ds(QUART, QUART)] += r1[p, 3]
        for copy in send2(i):
            copy.start()

    def stage3(i):
        p = lax.rem(i, RING)
        for copy in send2(i):
            copy.wait()
        quad[p, 0] = part[p, 0, x] + (r2[p, 0] + r2[p, 1])
        quad[p, 1] = part[p, 1, :, y] + (r2[p, 2] + r2[p, 3])
        for copy in send3(i):
            copy.start()

    def stage4(i):
        p = lax.rem(i, RING)
        for copy in send3(i):
            copy.wait()
        quad[p, 1, xp, pl.ds(0, QUART)] += r3[p, 0]
        quad[p, 1, xm, pl.ds(QUART, QUART)] += r3[p, 1]
        quad[p, 0, yp, pl.ds(0, QUART)] += r3[p, 2]
        quad[p, 0, ym, pl.ds(QUART, QUART)] += r3[p, 3]
        for copy in send4(i):
            copy.start()

    def stage5(i):
        p = lax.rem(i, RING)
        for copy in send4(i):
            copy.wait()
        done[i, :, pl.ds(0, LANES)] = quad[p, 0, y] + (r4[p, 2] + r4[p, 3])
        done[i, :, pl.ds(LANES, LANES)] = quad[p, 1, x] + (r4[p, 0] + r4[p, 1])

        @pl.when(i > Z_BEGIN - 4)
        def _():
            zstart(i)

    def step(i, carry):
        for k in range(2, NZ):
            pl.when(i == FETCH_AT[k])(functools.partial(fetch, k))
        for lag, stage in enumerate((stage1, stage2, stage3, stage4, stage5)):
            pl.when(jnp.logical_and(i >= lag, i < STEPS + lag))(functools.partial(stage, i - lag))
            if lag == 0:
                pl.when(i == FETCH_AT[1])(functools.partial(fetch, 1))

        @pl.when(i == LEG2_BEGIN)
        def _():
            for half in range(2):
                leg1(half).wait_recv()
                leg2(half).start()

        @pl.when(i == Z_BEGIN)
        def _():
            def begin(j, carry):
                zstart(j)
                return carry

            lax.fori_loop(0, Z_BEGIN - 3, begin, 0)

        @pl.when(i == Z_END)
        def _():
            for n in range(2):
                for h in range(PER):
                    if ready(n, h):
                        merge(n, h)

        return carry

    lax.fori_loop(0, STEPS + 4, step, 0)

    for n in range(2):
        for h in range(PER):
            if not ready(n, h):
                merge(n, h)
    drive_copy.wait()
    for h in range(PER):
        for n in range(2):
            last(n, h).wait_recv()
        cols = pl.ds(h * SUB, SUB)
        ladder = (done[AT[0, h]] + (fin[0, h] + fin[1, h])).T
        out[:, cols] = (drive[:, cols] + ladder) / denominator[:, cols]
    for n in range(2):
        for h in range(PER):
            last(n, h).wait_send()
    for k, d in enumerate(ORDER):
        if d not in (0, 1, 7):
            for h in range(PER):
                for n in zparts(k):
                    zsend(AT[k, h], k, h, n).wait_send()
    a_swap.wait_send()
    for k in range(1, NZ):
        forward(k).wait_send()
    for k in range(1, NZ):
        if k != FAR:
            a_send(k).wait_send()
    for half in range(2):
        leg1(half).wait_send()
        leg2(half).wait_send()


def update(amplitudes, integrals, driver, block_sizes, *tables):
    f32, bf16 = jnp.float32, jnp.bfloat16
    dma = pltpu.SemaphoreType.DMA
    scratch = [
        pltpu.VMEM((ROWS, COLS), f32), dma, pltpu.VMEM((ROWS, COLS), f32),
        pltpu.SMEM((NZ,), jnp.int32),
        *(pltpu.VMEM(table.shape, table.dtype) for table in tables),
        dma((len(tables) + 1,)),
        pltpu.VMEM((NZ, ROWS, KD), f32),
        pltpu.VMEM((NZ, ROWS, KD), f32),
        pltpu.VMEM((2, ROWS // 2, KD), f32),
        pltpu.VMEM((PER, NX * NX, SUB, KD), f32),
        pltpu.VMEM((PER, NX * NX, SUB, KD), f32),
        pltpu.VMEM((ROWS, 6 * KD), bf16),
        pltpu.VMEM((PER, NX * NX * SUB, 6 * KD), bf16),
        pltpu.VMEM((RING, 2, NX, NX, SUB, LANES), f32),
        pltpu.VMEM((RING, 2, NX, SUB, LANES), f32),
        pltpu.VMEM((STEPS, SUB, ROWS), f32),
        pltpu.VMEM((RING, 4, NX, QUART, LANES), f32),
        pltpu.VMEM((RING, 4, NX, SUB, LANES), f32),
        pltpu.VMEM((RING, 4, QUART, LANES), f32),
        pltpu.VMEM((RING, 4, SUB, LANES), f32),
        pltpu.VMEM((2, 2, PER, SUB, ROWS), f32),
        pltpu.VMEM((2, PER, QUART, ROWS), f32),
        pltpu.VMEM((2, PER, SUB, ROWS), f32),
        dma, dma((PER,)), dma((PER,)), dma((PER,)),
        dma((NZ,)), dma((NZ,)), dma((4,)), dma((4,)), dma((NZ,)), dma((NZ,)),
        dma((RING, 4)), dma((RING, 4)), dma((RING, 4)), dma((RING, 4)),
        dma((RING, 4)), dma((RING, 4)), dma((RING, 4)), dma((RING, 4)),
        dma((NZ, PER, 2)), dma((NZ, PER, 2)), dma((2, PER)), dma((2, PER)),
    ]
    return pl.pallas_call(
        ladder_kernel,
        out_shape=jax.ShapeDtypeStruct((ROWS, COLS), f32),
        in_specs=[pl.BlockSpec(memory_space=pltpu.HBM)] * (4 + len(tables)),
        out_specs=pl.BlockSpec(memory_space=pltpu.VMEM),
        scratch_shapes=scratch,
        compiler_params=pltpu.CompilerParams(
            collective_id=0, has_side_effects=True, vmem_limit_bytes=60 * 1024 * 1024
        ),
        cost_estimate=pl.CostEstimate(
            flops=3 * 2 * 2048 * 2048 * 768, bytes_accessed=12 * 1024 * 1024, transcendentals=0
        ),
        name="ladder",
    )(block_sizes, amplitudes, integrals.reshape(NX * NX, 2, COLS, KD), *tables, driver)


def body(
    amplitudes,
    integrals,
    driver,
    block_sizes,
    pair_first,
    pair_second,
    ab_first,
    ab_second,
    occ_energy,
    virt_energy,
):
    tables = (pair_first, pair_second, ab_first, ab_second, occ_energy, virt_energy)
    return update(amplitudes, integrals, driver, block_sizes, *(table[None] for table in tables))


def solution(mesh):
    placed = (
        P("pair", "slab"),
        P(None, ("slab", "pair")),
        P("pair", "slab"),
        P(),
        P("pair"),
        P("pair"),
        P("slab"),
        P("slab"),
        P(),
        P(),
    )
    return jax.shard_map(
        body, mesh=mesh, in_specs=placed, out_specs=P("pair", "slab"), check_vma=False
    )
```

```python
import functools

import jax
import jax.numpy as jnp
from jax import lax
from jax.experimental import pallas as pl
from jax.experimental.pallas import tpu as pltpu
from jax.sharding import PartitionSpec as P

MESH = pl.DeviceIdType.MESH
NN = (((1,), (0,)), ((), ()))

NZ = 8
NX = 4
ROWS = 256
KD = 384
COLS = 128
SUB = 64
PER = COLS // SUB
QUART = SUB // 2
STEPS = NZ * PER
LANES = 128
MROWS = 2 * NX * SUB
RING = 4
ORDER = (0, 1, 7, 2, 6, 3, 5, 4)
FAR = ORDER.index(4)
TABLE = [(0, h) for h in range(PER // 2)] + [(k, h) for k in range(1, NZ) for h in range(PER)]
TABLE += [(0, h) for h in range(PER // 2, PER)]
AT = {entry: i for i, entry in enumerate(TABLE)}
PART_AT = [min(i for i, entry in enumerate(TABLE) if entry[1] == h) for h in range(PER)]
BLOCK_AT = [i for i, entry in enumerate(TABLE) if i == 0 or TABLE[i - 1][0] != entry[0]]
FETCH_AT = [AT[k, 0] - 1 for k in range(NZ)]
FIRST = (1, 2)
SECOND = (3, 4)
A_BEGIN = ((2, (5, 6)),)
LEG1_BEGIN = 4
LEG2_BEGIN = 9
Z_BEGIN = 12
Z_END = STEPS + 2


def split(v):
    hi = v.astype(jnp.bfloat16)
    lo = (v - hi.astype(jnp.float32)).astype(jnp.bfloat16)
    return hi, lo


def ladder_kernel(
    sizes_hbm, a_hbm, b_hbm, pf_hbm, ps_hbm, af_hbm, as_hbm, occ_hbm, virt_hbm, drive_hbm, out,
    drive, drive_sem, denominator, sizes, pf, ps, af, asec, occ, virt, small_sem, a_own, a_sib, relay, b_own, b_sib, a3, b3, part, quad, done,
    r1, r2, r3, r4, mg, mh, fin,
    loc_sem, bl, bs, br, as_, ar, hs, hr, fs, fr, s1, q1, s2, q2, s3, q3, s4, q4, zs, zq, es, eq,
):
    z = lax.axis_index("pair")
    s = lax.axis_index("slab")
    x, y, c = s // (2 * NX), (s // 2) % NX, s % 2

    def slab(xx, yy, cc):
        return (xx * NX + yy) * 2 + cc

    def up(v, n, d):
        return lax.rem(v + d, n)

    xp, xo, xm = up(x, NX, 1), up(x, NX, 2), up(x, NX, 3)
    yp, yo, ym = up(y, NX, 1), up(y, NX, 2), up(y, NX, 3)
    sibling = (z, slab(x, y, 1 - c))
    side = ((z, slab(xp, y, c)), (z, slab(xm, y, c)), (z, slab(x, yp, c)), (z, slab(x, ym, c)))

    def zdev(d):
        return (up(z, NZ, d), s)

    def remote(src, dst, send, recv, dev):
        return pltpu.make_async_remote_copy(
            src_ref=src, dst_ref=dst, send_sem=send, recv_sem=recv, device_id=dev, device_id_type=MESH
        )

    barrier = pltpu.get_barrier_semaphore()
    peers = [sibling, *side] + [zdev(d) for d in range(1, NZ)]
    for dev in peers:
        pl.semaphore_signal(barrier, inc=1, device_id=dev, device_id_type=MESH)

    small = ((sizes_hbm, sizes), (pf_hbm, pf), (ps_hbm, ps), (af_hbm, af), (as_hbm, asec), (occ_hbm, occ), (virt_hbm, virt))
    small = [pltpu.make_async_copy(src, dst, small_sem.at[n]) for n, (src, dst) in enumerate(small)]

    def acols(d):
        return pl.ds(pl.multiple_of(up(z, NZ, d) * KD, KD), KD)

    def b_load(h):
        return pltpu.make_async_copy(b_hbm.at[:, c, pl.ds(h * SUB, SUB)], b_own.at[h], bl.at[h])

    def b_swap(h):
        return remote(b_hbm.at[:, 1 - c, pl.ds(h * SUB, SUB)], b_sib.at[h], bs.at[h], br.at[h], sibling)

    a_loc = pltpu.make_async_copy(a_hbm.at[:, acols(0)], a_own.at[0], loc_sem)
    a_swap = remote(a_hbm.at[:, acols(0)], a_sib.at[0], fs.at[0], fr.at[0], sibling)
    drive_copy = pltpu.make_async_copy(drive_hbm, drive, drive_sem)
    for copy in small:
        copy.start()
    b_load(0).start()
    a_loc.start()
    pl.semaphore_wait(barrier, len(peers))
    b_swap(0).start()
    a_swap.start()

    def a_send(k):
        d = NZ - ORDER[k]
        return remote(a_hbm.at[:, acols(d)], a_own.at[k], as_.at[k], ar.at[k], zdev(d))

    def leg1(h):
        rows = pl.ds(h * (ROWS // 2), ROWS // 2)
        return remote(a_hbm.at[rows, acols(4)], relay.at[h], hs.at[h], hr.at[h], zdev((2, 6)[h]))

    def leg2(h):
        rows = pl.ds(h * (ROWS // 2), ROWS // 2)
        return remote(relay.at[h], a_own.at[FAR, rows], hs.at[2 + h], hr.at[2 + h], zdev((2, 6)[h]))

    def forward(k):
        return remote(a_own.at[k], a_sib.at[k], fs.at[k], fr.at[k], sibling)

    for k in FIRST:
        a_send(k).start()
    drive_copy.start()
    small[0].wait()

    def looked_up(table, index, width):
        entry = lax.broadcasted_iota(jnp.int32, (table.shape[1], width), 0)
        hits = jnp.where(entry == index[...], 1.0, 0.0).astype(jnp.bfloat16)
        row = jnp.broadcast_to(table[...], (8, table.shape[1]))
        hi = row.astype(jnp.bfloat16).astype(jnp.float32)
        mid = (row - hi).astype(jnp.bfloat16).astype(jnp.float32)
        term = lax.broadcasted_iota(jnp.int32, row.shape, 0)
        terms = jnp.where(term == 0, hi, jnp.where(term == 1, mid, row - hi - mid)).astype(jnp.bfloat16)
        got = lax.dot_general(terms, hits, (((1,), (0,)), ((), ())), preferred_element_type=jnp.float32)
        return got[0:1] + (got[1:2] + got[2:3])

    def energies():
        for copy in small[1:]:
            copy.wait()
        occupied = looked_up(occ, pf, ROWS) + looked_up(occ, ps, ROWS)
        rows = jnp.broadcast_to(occupied, (COLS, ROWS)).T
        first, second = looked_up(virt, af, COLS), looked_up(virt, asec, COLS)
        denominator[...] = (rows - first) - second

    energies()

    limit = sizes[s // 4]
    column = lax.broadcasted_iota(jnp.int32, (SUB, KD), 1)

    def convert(src, h, first, slab_at):
        live = column < limit - (slab_at % 4) * (NZ * KD) - z * KD

        def one(j, carry):
            hi, lo = split(jnp.where(live, src[h, j], 0.0))
            rows = pl.ds(pl.multiple_of(j * SUB, SUB), SUB)
            b3[h, rows, pl.ds(first, KD)] = hi
            b3[h, rows, pl.ds(2 * KD + first, KD)] = lo
            b3[h, rows, pl.ds(4 * KD + first, KD)] = hi
            return carry

        lax.fori_loop(0, NX * NX, one, 0)

    def send1(i):
        p = lax.rem(i, RING)
        src = (
            part.at[p, 0, xo, :, pl.ds(0, QUART)],
            part.at[p, 0, xo, :, pl.ds(QUART, QUART)],
            part.at[p, 1, :, yo, pl.ds(0, QUART)],
            part.at[p, 1, :, yo, pl.ds(QUART, QUART)],
        )
        return [remote(src[k], r1.at[p, k], s1.at[p, k], q1.at[p, k], side[k]) for k in range(4)]

    def send2(i):
        p = lax.rem(i, RING)
        src = (part.at[p, 0, xp], part.at[p, 0, xm], part.at[p, 1, :, yp], part.at[p, 1, :, ym])
        return [remote(src[k], r2.at[p, k], s2.at[p, k], q2.at[p, k], side[k]) for k in range(4)]

    def send3(i):
        p = lax.rem(i, RING)
        src = (
            quad.at[p, 1, xo, pl.ds(0, QUART)],
            quad.at[p, 1, xo, pl.ds(QUART, QUART)],
            quad.at[p, 0, yo, pl.ds(0, QUART)],
            quad.at[p, 0, yo, pl.ds(QUART, QUART)],
        )
        return [remote(src[k], r3.at[p, k], s3.at[p, k], q3.at[p, k], side[k]) for k in range(4)]

    def send4(i):
        p = lax.rem(i, RING)
        src = (quad.at[p, 1, xp], quad.at[p, 1, xm], quad.at[p, 0, yp], quad.at[p, 0, ym])
        return [remote(src[k], r4.at[p, k], s4.at[p, k], q4.at[p, k], side[k]) for k in range(4)]

    def zparts(k):
        return range(2 if k == FAR else 1)

    def zsend(i, k, h, part_at):
        d = ORDER[k]
        if d == 4:
            src, dst, dev = done.at[i, pl.ds(part_at * QUART, QUART)], mh.at[part_at, h], zdev(3 + 2 * part_at)
        elif d < 4:
            src, dst, dev = done.at[i], mg.at[0, d - 2, h], zdev(d - 1)
        else:
            src, dst, dev = done.at[i], mg.at[1, 6 - d, h], zdev(d + 1)
        return remote(src, dst, zs.at[k, h, part_at], zq.at[k, h, part_at], dev)

    def entry(i):
        k = sum(jnp.where(i == at, block, 0) for at, (block, h) in enumerate(TABLE))
        return k, sum(jnp.where(i == at, h, 0) for at, (block, h) in enumerate(TABLE))

    def zstart(i):
        block, h = entry(i)
        for k, d in enumerate(ORDER):
            if d not in (0, 1, 7):
                @pl.when(block == k)
                def _():
                    for n in zparts(k):
                        zsend(i, k, h, n).start()

    def last(n, h):
        i = AT[ORDER.index((1, 7)[n]), h]
        return remote(done.at[i], fin.at[n, h], es.at[n, h], eq.at[n, h], zdev((1, 7)[n]))

    def merge(n, h):
        for d in ((2, 3), (6, 5))[n]:
            k = ORDER.index(d)
            zsend(AT[k, h], k, h, 0).wait_recv()
        zsend(AT[FAR, h], FAR, h, n).wait_recv()
        i = AT[ORDER.index((1, 7)[n]), h]
        done[i] += mg[n, 0, h] + mg[n, 1, h]
        done[i, pl.ds(n * QUART, QUART)] += mh[n, h]
        last(n, h).start()

    def ready(n, h):
        return max(AT[ORDER.index((1, 7)[n]), h], AT[FAR, h]) + 5 <= Z_END

    def stage1(i):
        p = lax.rem(i, RING)
        k, h = entry(i)

        for step_at in range(PER):
            @pl.when(i == PART_AT[step_at])
            def _():
                b_load(step_at).wait()
                convert(b_own, step_at, 0, s)
                if step_at == 0:
                    a_loc.wait()
                    for kk in SECOND:
                        a_send(kk).start()
                b_swap(step_at).wait()
                convert(b_sib, step_at, KD, slab(x, y, 1 - c))
                if step_at + 1 < PER:
                    b_swap(step_at + 1).start()
                    b_load(step_at + 1).start()

        @pl.when(functools.reduce(jnp.logical_or, [i == at for at in BLOCK_AT[:-1]]))
        def _():
            forward(k).wait_recv()

        @pl.when(functools.reduce(jnp.logical_or, [i == at for at in BLOCK_AT]))
        def _():
            for first, source in ((0, a_own), (KD, a_sib)):
                hi, lo = split(source[k].T)
                a3[pl.ds(first, KD), :] = hi
                a3[pl.ds(2 * KD + first, KD), :] = hi
                a3[pl.ds(4 * KD + first, KD), :] = lo

        def columns(m, carry):
            rows = pl.ds(pl.multiple_of(m * MROWS, MROWS), MROWS)
            acc = lax.dot_general(b3[h, rows, :], a3[...], NN, preferred_element_type=jnp.float32)
            for xx in range(2):
                for yy in range(NX):
                    at = (xx * NX + yy) * SUB
                    for half in range(2):
                        part[p, half, 2 * m + xx, yy] = acc[at:at + SUB, half * LANES:(half + 1) * LANES]
            return carry

        lax.fori_loop(0, NX // 2, columns, 0)
        for copy in send1(i):
            copy.start()

        for begin, blocks in A_BEGIN:
            @pl.when(i == begin)
            def _():
                for kk in blocks:
                    a_send(kk).start()

        @pl.when(i == LEG1_BEGIN)
        def _():
            for half in range(2):
                leg1(half).start()

    def fetch(k):
        if k == FAR:
            for half in range(2):
                leg2(half).wait_recv()
        else:
            a_send(k).wait_recv()
        forward(k).start()

    def stage2(i):
        p = lax.rem(i, RING)
        for copy in send1(i):
            copy.wait()
        part[p, 0, xp, :, pl.ds(0, QUART)] += r1[p, 0]
        part[p, 0, xm, :, pl.ds(QUART, QUART)] += r1[p, 1]
        part[p, 1, :, yp, pl.ds(0, QUART)] += r1[p, 2]
        part[p, 1, :, ym, pl.ds(QUART, QUART)] += r1[p, 3]
        for copy in send2(i):
            copy.start()

    def stage3(i):
        p = lax.rem(i, RING)
        for copy in send2(i):
            copy.wait()
        quad[p, 0] = part[p, 0, x] + (r2[p, 0] + r2[p, 1])
        quad[p, 1] = part[p, 1, :, y] + (r2[p, 2] + r2[p, 3])
        for copy in send3(i):
            copy.start()

    def stage4(i):
        p = lax.rem(i, RING)
        for copy in send3(i):
            copy.wait()
        quad[p, 1, xp, pl.ds(0, QUART)] += r3[p, 0]
        quad[p, 1, xm, pl.ds(QUART, QUART)] += r3[p, 1]
        quad[p, 0, yp, pl.ds(0, QUART)] += r3[p, 2]
        quad[p, 0, ym, pl.ds(QUART, QUART)] += r3[p, 3]
        for copy in send4(i):
            copy.start()

    def stage5(i):
        p = lax.rem(i, RING)
        for copy in send4(i):
            copy.wait()
        done[i, :, pl.ds(0, LANES)] = quad[p, 0, y] + (r4[p, 2] + r4[p, 3])
        done[i, :, pl.ds(LANES, LANES)] = quad[p, 1, x] + (r4[p, 0] + r4[p, 1])

        @pl.when(i > Z_BEGIN - 4)
        def _():
            zstart(i)

    def step(i, carry):
        for k in range(2, NZ):
            pl.when(i == FETCH_AT[k])(functools.partial(fetch, k))
        for lag, stage in enumerate((stage1, stage2, stage3, stage4, stage5)):
            pl.when(jnp.logical_and(i >= lag, i < STEPS + lag))(functools.partial(stage, i - lag))
            if lag == 0:
                pl.when(i == FETCH_AT[1])(functools.partial(fetch, 1))

        @pl.when(i == LEG2_BEGIN)
        def _():
            for half in range(2):
                leg1(half).wait_recv()
                leg2(half).start()

        @pl.when(i == Z_BEGIN)
        def _():
            def begin(j, carry):
                zstart(j)
                return carry

            lax.fori_loop(0, Z_BEGIN - 3, begin, 0)

        @pl.when(i == Z_END)
        def _():
            for n in range(2):
                for h in range(PER):
                    if ready(n, h):
                        merge(n, h)

        return carry

    lax.fori_loop(0, STEPS + 4, step, 0)

    for n in range(2):
        for h in range(PER):
            if not ready(n, h):
                merge(n, h)
    drive_copy.wait()
    for h in range(PER):
        for n in range(2):
            last(n, h).wait_recv()
        cols = pl.ds(h * SUB, SUB)
        ladder = (done[AT[0, h]] + (fin[0, h] + fin[1, h])).T
        out[:, cols] = (drive[:, cols] + ladder) / denominator[:, cols]
    for n in range(2):
        for h in range(PER):
            last(n, h).wait_send()
    for k, d in enumerate(ORDER):
        if d not in (0, 1, 7):
            for h in range(PER):
                for n in zparts(k):
                    zsend(AT[k, h], k, h, n).wait_send()
    a_swap.wait_send()
    for k in range(1, NZ):
        forward(k).wait_send()
    for k in range(1, NZ):
        if k != FAR:
            a_send(k).wait_send()
    for half in range(2):
        leg1(half).wait_send()
        leg2(half).wait_send()


def update(amplitudes, integrals, driver, block_sizes, *tables):
    f32, bf16 = jnp.float32, jnp.bfloat16
    dma = pltpu.SemaphoreType.DMA
    scratch = [
        pltpu.VMEM((ROWS, COLS), f32), dma, pltpu.VMEM((ROWS, COLS), f32),
        pltpu.SMEM((NZ,), jnp.int32),
        *(pltpu.VMEM(table.shape, table.dtype) for table in tables),
        dma((len(tables) + 1,)),
        pltpu.VMEM((NZ, ROWS, KD), f32),
        pltpu.VMEM((NZ, ROWS, KD), f32),
        pltpu.VMEM((2, ROWS // 2, KD), f32),
        pltpu.VMEM((PER, NX * NX, SUB, KD), f32),
        pltpu.VMEM((PER, NX * NX, SUB, KD), f32),
        pltpu.VMEM((6 * KD, ROWS), bf16),
        pltpu.VMEM((PER, NX * NX * SUB, 6 * KD), bf16),
        pltpu.VMEM((RING, 2, NX, NX, SUB, LANES), f32),
        pltpu.VMEM((RING, 2, NX, SUB, LANES), f32),
        pltpu.VMEM((STEPS, SUB, ROWS), f32),
        pltpu.VMEM((RING, 4, NX, QUART, LANES), f32),
        pltpu.VMEM((RING, 4, NX, SUB, LANES), f32),
        pltpu.VMEM((RING, 4, QUART, LANES), f32),
        pltpu.VMEM((RING, 4, SUB, LANES), f32),
        pltpu.VMEM((2, 2, PER, SUB, ROWS), f32),
        pltpu.VMEM((2, PER, QUART, ROWS), f32),
        pltpu.VMEM((2, PER, SUB, ROWS), f32),
        dma, dma((PER,)), dma((PER,)), dma((PER,)),
        dma((NZ,)), dma((NZ,)), dma((4,)), dma((4,)), dma((NZ,)), dma((NZ,)),
        dma((RING, 4)), dma((RING, 4)), dma((RING, 4)), dma((RING, 4)),
        dma((RING, 4)), dma((RING, 4)), dma((RING, 4)), dma((RING, 4)),
        dma((NZ, PER, 2)), dma((NZ, PER, 2)), dma((2, PER)), dma((2, PER)),
    ]
    return pl.pallas_call(
        ladder_kernel,
        out_shape=jax.ShapeDtypeStruct((ROWS, COLS), f32),
        in_specs=[pl.BlockSpec(memory_space=pltpu.HBM)] * (4 + len(tables)),
        out_specs=pl.BlockSpec(memory_space=pltpu.VMEM),
        scratch_shapes=scratch,
        compiler_params=pltpu.CompilerParams(
            collective_id=0, has_side_effects=True, vmem_limit_bytes=60 * 1024 * 1024
        ),
        cost_estimate=pl.CostEstimate(
            flops=3 * 2 * 2048 * 2048 * 768, bytes_accessed=12 * 1024 * 1024, transcendentals=0
        ),
        name="ladder",
    )(block_sizes, amplitudes, integrals.reshape(NX * NX, 2, COLS, KD), *tables, driver)


def body(
    amplitudes,
    integrals,
    driver,
    block_sizes,
    pair_first,
    pair_second,
    ab_first,
    ab_second,
    occ_energy,
    virt_energy,
):
    tables = (pair_first, pair_second, ab_first, ab_second, occ_energy, virt_energy)
    return update(amplitudes, integrals, driver, block_sizes, *(table[None] for table in tables))


def solution(mesh):
    placed = (
        P("pair", "slab"),
        P(None, ("slab", "pair")),
        P("pair", "slab"),
        P(),
        P("pair"),
        P("pair"),
        P("slab"),
        P("slab"),
        P(),
        P(),
    )
    return jax.shard_map(
        body, mesh=mesh, in_specs=placed, out_specs=P("pair", "slab"), check_vma=False
    )
```

```python
import functools

import jax
import jax.numpy as jnp
from jax import lax
from jax.experimental import pallas as pl
from jax.experimental.pallas import tpu as pltpu
from jax.sharding import PartitionSpec as P

MESH = pl.DeviceIdType.MESH
NT = (((1,), (1,)), ((), ()))

NZ = 8
NX = 4
ROWS = 256
KD = 384
COLS = 128
SUB = 32
PER = COLS // SUB
QUART = SUB // 2
STEPS = NZ * PER
LANES = 128
XS = 4
MROWS = XS * NX * SUB
RING = 8
LAGS = (0, 2, 4)
LAG = LAGS[2] + 1
END = LAG + LAGS[2]
ORDER = (0, 1, 7, 2, 6, 3, 5, 4)
FAR = ORDER.index(4)
TABLE = [(0, h) for h in range(PER // 2)] + [(k, h) for k in range(1, NZ) for h in range(PER)]
TABLE += [(0, h) for h in range(PER // 2, PER)]
AT = {entry: i for i, entry in enumerate(TABLE)}
PART_AT = [min(i for i, entry in enumerate(TABLE) if entry[1] == h) for h in range(PER)]
BLOCK_AT = [i for i, entry in enumerate(TABLE) if i == 0 or TABLE[i - 1][0] != entry[0]]
FETCH_AT = [AT[k, 0] - PER // 2 for k in range(NZ)]
FIRST = (1, 2)
SECOND = (3, 4)
A_BEGIN = ((4, (5, 6)),)
LEG1_BEGIN = 8
LEG2_BEGIN = 18
Z_BEGIN = 27
Z_END = STEPS + END - 2


def split(v):
    hi = v.astype(jnp.bfloat16)
    lo = (v - hi.astype(jnp.float32)).astype(jnp.bfloat16)
    return hi, lo


def ladder_kernel(
    sizes_hbm, a_hbm, b_hbm, pf_hbm, ps_hbm, af_hbm, as_hbm, occ_hbm, virt_hbm, drive_hbm, out,
    drive, drive_sem, denominator, sizes, pf, ps, af, asec, occ, virt, small_sem, a_own, a_sib, relay, b_own, b_sib, a3, b3, part, quad, done,
    o1, o2, r1, r2, mg, mh, fin,
    loc_sem, bl, bs, br, as_, ar, hs, hr, fs, fr, s1, q1, s2, q2, zs, zq, es, eq,
):
    z = lax.axis_index("pair")
    s = lax.axis_index("slab")
    x, y, c = s // (2 * NX), (s // 2) % NX, s % 2

    def slab(xx, yy, cc):
        return (xx * NX + yy) * 2 + cc

    def up(v, n, d):
        return lax.rem(v + d, n)

    xp, xo, xm = up(x, NX, 1), up(x, NX, 2), up(x, NX, 3)
    yp, yo, ym = up(y, NX, 1), up(y, NX, 2), up(y, NX, 3)
    sibling = (z, slab(x, y, 1 - c))
    side = ((z, slab(xp, y, c)), (z, slab(xm, y, c)), (z, slab(x, yp, c)), (z, slab(x, ym, c)))

    def zdev(d):
        return (up(z, NZ, d), s)

    def remote(src, dst, send, recv, dev):
        return pltpu.make_async_remote_copy(
            src_ref=src, dst_ref=dst, send_sem=send, recv_sem=recv, device_id=dev, device_id_type=MESH
        )

    barrier = pltpu.get_barrier_semaphore()
    peers = [sibling, *side] + [zdev(d) for d in range(1, NZ)]
    for dev in peers:
        pl.semaphore_signal(barrier, inc=1, device_id=dev, device_id_type=MESH)

    small = ((sizes_hbm, sizes), (pf_hbm, pf), (ps_hbm, ps), (af_hbm, af), (as_hbm, asec), (occ_hbm, occ), (virt_hbm, virt))
    small = [pltpu.make_async_copy(src, dst, small_sem.at[n]) for n, (src, dst) in enumerate(small)]

    def acols(d):
        return pl.ds(pl.multiple_of(up(z, NZ, d) * KD, KD), KD)

    def b_load(h):
        return pltpu.make_async_copy(b_hbm.at[:, c, pl.ds(h * SUB, SUB)], b_own.at[h], bl.at[h])

    def b_swap(h):
        return remote(b_hbm.at[:, 1 - c, pl.ds(h * SUB, SUB)], b_sib.at[h], bs.at[h], br.at[h], sibling)

    a_loc = pltpu.make_async_copy(a_hbm.at[:, acols(0)], a_own.at[0], loc_sem)
    a_swap = remote(a_hbm.at[:, acols(0)], a_sib.at[0], fs.at[0], fr.at[0], sibling)
    drive_copy = pltpu.make_async_copy(drive_hbm, drive, drive_sem)
    for copy in small:
        copy.start()
    for h in range(PER // 2):
        b_load(h).start()
    a_loc.start()
    pl.semaphore_wait(barrier, len(peers))
    b_swap(0).start()
    a_swap.start()
    for h in range(1, PER // 2):
        b_swap(h).start()

    def a_send(k):
        d = NZ - ORDER[k]
        return remote(a_hbm.at[:, acols(d)], a_own.at[k], as_.at[k], ar.at[k], zdev(d))

    def leg1(h):
        rows = pl.ds(h * (ROWS // 2), ROWS // 2)
        return remote(a_hbm.at[rows, acols(4)], relay.at[h], hs.at[h], hr.at[h], zdev((2, 6)[h]))

    def leg2(h):
        rows = pl.ds(h * (ROWS // 2), ROWS // 2)
        return remote(relay.at[h], a_own.at[FAR, rows], hs.at[2 + h], hr.at[2 + h], zdev((2, 6)[h]))

    def forward(k):
        return remote(a_own.at[k], a_sib.at[k], fs.at[k], fr.at[k], sibling)

    for k in FIRST:
        a_send(k).start()
    drive_copy.start()
    small[0].wait()

    def looked_up(table, index, width):
        entry = lax.broadcasted_iota(jnp.int32, (table.shape[1], width), 0)
        hits = jnp.where(entry == index[...], 1.0, 0.0).astype(jnp.bfloat16)
        row = jnp.broadcast_to(table[...], (8, table.shape[1]))
        hi = row.astype(jnp.bfloat16).astype(jnp.float32)
        mid = (row - hi).astype(jnp.bfloat16).astype(jnp.float32)
        term = lax.broadcasted_iota(jnp.int32, row.shape, 0)
        terms = jnp.where(term == 0, hi, jnp.where(term == 1, mid, row - hi - mid)).astype(jnp.bfloat16)
        got = lax.dot_general(terms, hits, (((1,), (0,)), ((), ())), preferred_element_type=jnp.float32)
        return got[0:1] + (got[1:2] + got[2:3])

    def energies():
        for copy in small[1:]:
            copy.wait()
        occupied = looked_up(occ, pf, ROWS) + looked_up(occ, ps, ROWS)
        rows = jnp.broadcast_to(occupied, (COLS, ROWS)).T
        first, second = looked_up(virt, af, COLS), looked_up(virt, asec, COLS)
        denominator[...] = (rows - first) - second

    energies()

    limit = sizes[s // 4]
    column = lax.broadcasted_iota(jnp.int32, (SUB, KD), 1)

    def convert(src, h, first, slab_at):
        live = column < limit - (slab_at % 4) * (NZ * KD) - z * KD

        def one(j, carry):
            hi, lo = split(jnp.where(live, src[h, j], 0.0))
            rows = pl.ds(pl.multiple_of(j * SUB, SUB), SUB)
            b3[h, rows, pl.ds(first, KD)] = hi
            b3[h, rows, pl.ds(2 * KD + first, KD)] = lo
            b3[h, rows, pl.ds(4 * KD + first, KD)] = hi
            return carry

        lax.fori_loop(0, NX * NX, one, 0)

    def send1(j, whole):
        p = lax.rem(j, RING)
        at = (lambda ref, k: ref.at[p, k]) if whole else (lambda ref, k: ref.at[p, k, NX])
        return [remote(at(o1, k), at(r1, k), s1.at[p, k], q1.at[p, k], side[k]) for k in range(4)]

    def send2(j, whole):
        p = lax.rem(j, RING)
        at = (lambda ref, k: ref.at[p, k]) if whole else (lambda ref, k: ref.at[p, k, NX])
        return [remote(at(o2, k), at(r2, k), s2.at[p, k], q2.at[p, k], side[k]) for k in range(4)]

    def copies(send, j, act):
        @pl.when(j < STEPS)
        def _():
            for copy in send(j, True):
                act(copy)

        @pl.when(j >= STEPS)
        def _():
            for copy in send(j, False):
                act(copy)

    def zparts(k):
        return range(2 if k == FAR else 1)

    def zsend(i, k, h, part_at):
        d = ORDER[k]
        if d == 4:
            src, dst, dev = done.at[i, pl.ds(part_at * QUART, QUART)], mh.at[part_at, h], zdev(3 + 2 * part_at)
        elif d < 4:
            src, dst, dev = done.at[i], mg.at[0, d - 2, h], zdev(d - 1)
        else:
            src, dst, dev = done.at[i], mg.at[1, 6 - d, h], zdev(d + 1)
        return remote(src, dst, zs.at[k, h, part_at], zq.at[k, h, part_at], dev)

    def entry(i):
        k = sum(jnp.where(i == at, block, 0) for at, (block, h) in enumerate(TABLE))
        return k, sum(jnp.where(i == at, h, 0) for at, (block, h) in enumerate(TABLE))

    def zstart(i):
        block, h = entry(i)
        for k, d in enumerate(ORDER):
            if d not in (0, 1, 7):
                @pl.when(block == k)
                def _():
                    for n in zparts(k):
                        zsend(i, k, h, n).start()

    def last(n, h):
        i = AT[ORDER.index((1, 7)[n]), h]
        return remote(done.at[i], fin.at[n, h], es.at[n, h], eq.at[n, h], zdev((1, 7)[n]))

    def merge(n, h):
        for d in ((2, 3), (6, 5))[n]:
            k = ORDER.index(d)
            zsend(AT[k, h], k, h, 0).wait_recv()
        zsend(AT[FAR, h], FAR, h, n).wait_recv()
        i = AT[ORDER.index((1, 7)[n]), h]
        done[i] += mg[n, 0, h] + mg[n, 1, h]
        done[i, pl.ds(n * QUART, QUART)] += mh[n, h]
        last(n, h).start()

    def ready(n, h):
        return max(AT[ORDER.index((1, 7)[n]), h], AT[FAR, h]) + END + 1 <= Z_END

    def dots(i):
        p = lax.rem(i, RING)
        k, h = entry(i)

        for step_at in range(PER):
            @pl.when(i == PART_AT[step_at])
            def _():
                b_load(step_at).wait()
                convert(b_own, step_at, 0, s)
                if step_at == 0:
                    a_loc.wait()
                    for kk in SECOND:
                        a_send(kk).start()
                b_swap(step_at).wait()
                convert(b_sib, step_at, KD, slab(x, y, 1 - c))
                if step_at + PER // 2 < PER:
                    b_swap(step_at + PER // 2).start()
                    b_load(step_at + PER // 2).start()

        @pl.when(functools.reduce(jnp.logical_or, [i == at for at in BLOCK_AT[:-1]]))
        def _():
            forward(k).wait_recv()

        @pl.when(functools.reduce(jnp.logical_or, [i == at for at in BLOCK_AT]))
        def _():
            for first, source in ((0, a_own), (KD, a_sib)):
                hi, lo = split(source[k])
                a3[:, pl.ds(first, KD)] = hi
                a3[:, pl.ds(2 * KD + first, KD)] = hi
                a3[:, pl.ds(4 * KD + first, KD)] = lo

        def columns(m, carry):
            rows = pl.ds(pl.multiple_of(m * MROWS, MROWS), MROWS)
            acc = lax.dot_general(b3[h, rows, :], a3[...], NT, preferred_element_type=jnp.float32)
            for xx in range(XS):
                for yy in range(NX):
                    at = (xx * NX + yy) * SUB
                    for half in range(2):
                        part[p, half, XS * m + xx, yy] = acc[at:at + SUB, half * LANES:(half + 1) * LANES]
            return carry

        lax.fori_loop(0, NX // XS, columns, 0)
        o1[p, 0, pl.ds(0, NX)] = part[p, 0, xo, :, pl.ds(0, QUART)]
        o1[p, 1, pl.ds(0, NX)] = part[p, 0, xo, :, pl.ds(QUART, QUART)]
        o1[p, 2, pl.ds(0, NX)] = part[p, 1, :, yo, pl.ds(0, QUART)]
        o1[p, 3, pl.ds(0, NX)] = part[p, 1, :, yo, pl.ds(QUART, QUART)]

    def boxes1(j):
        p, old = lax.rem(j, RING), lax.rem(j + RING - LAG, RING)
        pl.when(j < STEPS)(functools.partial(dots, j))

        @pl.when(j >= LAG)
        def _():
            o1[p, 0, NX] = quad[old, 1, xo, pl.ds(0, QUART)]
            o1[p, 1, NX] = quad[old, 1, xo, pl.ds(QUART, QUART)]
            o1[p, 2, NX] = quad[old, 0, yo, pl.ds(0, QUART)]
            o1[p, 3, NX] = quad[old, 0, yo, pl.ds(QUART, QUART)]

        copies(send1, j, lambda copy: copy.start())

    def begin_z(i):
        for begin, blocks in A_BEGIN:
            @pl.when(i == begin)
            def _():
                for kk in blocks:
                    a_send(kk).start()

        @pl.when(i == LEG1_BEGIN)
        def _():
            for half in range(2):
                leg1(half).start()

    def fetch(k):
        if k == FAR:
            for half in range(2):
                leg2(half).wait_recv()
        else:
            a_send(k).wait_recv()
        forward(k).start()

    low, high = pl.ds(0, QUART), pl.ds(QUART, QUART)

    def boxes2(j):
        p, old = lax.rem(j, RING), lax.rem(j + RING - LAG, RING)
        copies(send1, j, lambda copy: copy.wait())

        @pl.when(j < STEPS)
        def _():
            n = pl.ds(0, NX)
            o2[p, 0, n, low] = part[p, 0, xp, :, low] + r1[p, 0, n]
            o2[p, 0, n, high] = part[p, 0, xp, :, high]
            o2[p, 1, n, low] = part[p, 0, xm, :, low]
            o2[p, 1, n, high] = part[p, 0, xm, :, high] + r1[p, 1, n]
            o2[p, 2, n, low] = part[p, 1, :, yp, low] + r1[p, 2, n]
            o2[p, 2, n, high] = part[p, 1, :, yp, high]
            o2[p, 3, n, low] = part[p, 1, :, ym, low]
            o2[p, 3, n, high] = part[p, 1, :, ym, high] + r1[p, 3, n]

        @pl.when(j >= LAG)
        def _():
            for k, half, to in ((0, 1, xp), (1, 1, xm), (2, 0, yp), (3, 0, ym)):
                plus, plain = (low, high) if k % 2 == 0 else (high, low)
                o2[p, k, NX, plus] = quad[old, half, to, plus] + r1[p, k, NX]
                o2[p, k, NX, plain] = quad[old, half, to, plain]

        copies(send2, j, lambda copy: copy.start())

    def sums(j):
        p, old = lax.rem(j, RING), lax.rem(j + RING - LAG, RING)
        copies(send2, j, lambda copy: copy.wait())

        @pl.when(j < STEPS)
        def _():
            n = pl.ds(0, NX)
            quad[p, 0] = part[p, 0, x] + (r2[p, 0, n] + r2[p, 1, n])
            quad[p, 1] = part[p, 1, :, y] + (r2[p, 2, n] + r2[p, 3, n])

        @pl.when(j >= LAG)
        def _():
            done[j - LAG, :, pl.ds(0, LANES)] = quad[old, 0, y] + (r2[p, 2, NX] + r2[p, 3, NX])
            done[j - LAG, :, pl.ds(LANES, LANES)] = quad[old, 1, x] + (r2[p, 0, NX] + r2[p, 1, NX])

            @pl.when(j - LAG > Z_BEGIN - END)
            def _():
                zstart(j - LAG)

    def step(i, carry):
        for k in range(2, NZ):
            pl.when(i == FETCH_AT[k])(functools.partial(fetch, k))
        for lag, stage in zip(LAGS, (boxes1, boxes2, sums)):
            pl.when(jnp.logical_and(i >= lag, i < STEPS + LAG + lag))(functools.partial(stage, i - lag))
            if lag == 0:
                begin_z(i)
                pl.when(i == FETCH_AT[1])(functools.partial(fetch, 1))

        @pl.when(i == LEG2_BEGIN)
        def _():
            for half in range(2):
                leg1(half).wait_recv()
                leg2(half).start()

        @pl.when(i == Z_BEGIN)
        def _():
            def begin(j, carry):
                zstart(j)
                return carry

            lax.fori_loop(0, Z_BEGIN - END + 1, begin, 0)

        @pl.when(i == Z_END)
        def _():
            for n in range(2):
                for h in range(PER):
                    if ready(n, h):
                        merge(n, h)

        return carry

    lax.fori_loop(0, STEPS + END, step, 0)

    for n in range(2):
        for h in range(PER):
            if not ready(n, h):
                merge(n, h)
    drive_copy.wait()
    for h in range(PER):
        for n in range(2):
            last(n, h).wait_recv()
        cols = pl.ds(h * SUB, SUB)
        ladder = (done[AT[0, h]] + (fin[0, h] + fin[1, h])).T
        out[:, cols] = (drive[:, cols] + ladder) / denominator[:, cols]
    for n in range(2):
        for h in range(PER):
            last(n, h).wait_send()
    for k, d in enumerate(ORDER):
        if d not in (0, 1, 7):
            for h in range(PER):
                for n in zparts(k):
                    zsend(AT[k, h], k, h, n).wait_send()
    a_swap.wait_send()
    for k in range(1, NZ):
        forward(k).wait_send()
    for k in range(1, NZ):
        if k != FAR:
            a_send(k).wait_send()
    for half in range(2):
        leg1(half).wait_send()
        leg2(half).wait_send()


def update(amplitudes, integrals, driver, block_sizes, *tables):
    f32, bf16 = jnp.float32, jnp.bfloat16
    dma = pltpu.SemaphoreType.DMA
    scratch = [
        pltpu.VMEM((ROWS, COLS), f32), dma, pltpu.VMEM((ROWS, COLS), f32),
        pltpu.SMEM((NZ,), jnp.int32),
        *(pltpu.VMEM(table.shape, table.dtype) for table in tables),
        dma((len(tables) + 1,)),
        pltpu.VMEM((NZ, ROWS, KD), f32),
        pltpu.VMEM((NZ, ROWS, KD), f32),
        pltpu.VMEM((2, ROWS // 2, KD), f32),
        pltpu.VMEM((PER, NX * NX, SUB, KD), f32),
        pltpu.VMEM((PER, NX * NX, SUB, KD), f32),
        pltpu.VMEM((ROWS, 6 * KD), bf16),
        pltpu.VMEM((PER, NX * NX * SUB, 6 * KD), bf16),
        pltpu.VMEM((RING, 2, NX, NX, SUB, LANES), f32),
        pltpu.VMEM((RING, 2, NX, SUB, LANES), f32),
        pltpu.VMEM((STEPS, SUB, ROWS), f32),
        pltpu.VMEM((RING, 4, NX + 1, QUART, LANES), f32),
        pltpu.VMEM((RING, 4, NX + 1, SUB, LANES), f32),
        pltpu.VMEM((RING, 4, NX + 1, QUART, LANES), f32),
        pltpu.VMEM((RING, 4, NX + 1, SUB, LANES), f32),
        pltpu.VMEM((2, 2, PER, SUB, ROWS), f32),
        pltpu.VMEM((2, PER, QUART, ROWS), f32),
        pltpu.VMEM((2, PER, SUB, ROWS), f32),
        dma, dma((PER,)), dma((PER,)), dma((PER,)),
        dma((NZ,)), dma((NZ,)), dma((4,)), dma((4,)), dma((NZ,)), dma((NZ,)),
        dma((RING, 4)), dma((RING, 4)), dma((RING, 4)), dma((RING, 4)),
        dma((NZ, PER, 2)), dma((NZ, PER, 2)), dma((2, PER)), dma((2, PER)),
    ]
    return pl.pallas_call(
        ladder_kernel,
        out_shape=jax.ShapeDtypeStruct((ROWS, COLS), f32),
        in_specs=[pl.BlockSpec(memory_space=pltpu.HBM)] * (4 + len(tables)),
        out_specs=pl.BlockSpec(memory_space=pltpu.VMEM),
        scratch_shapes=scratch,
        compiler_params=pltpu.CompilerParams(
            collective_id=0, has_side_effects=True, vmem_limit_bytes=60 * 1024 * 1024
        ),
        cost_estimate=pl.CostEstimate(
            flops=3 * 2 * 2048 * 2048 * 768, bytes_accessed=12 * 1024 * 1024, transcendentals=0
        ),
        name="ladder",
    )(block_sizes, amplitudes, integrals.reshape(NX * NX, 2, COLS, KD), *tables, driver)


def body(
    amplitudes,
    integrals,
    driver,
    block_sizes,
    pair_first,
    pair_second,
    ab_first,
    ab_second,
    occ_energy,
    virt_energy,
):
    tables = (pair_first, pair_second, ab_first, ab_second, occ_energy, virt_energy)
    return update(amplitudes, integrals, driver, block_sizes, *(table[None] for table in tables))


def solution(mesh):
    placed = (
        P("pair", "slab"),
        P(None, ("slab", "pair")),
        P("pair", "slab"),
        P(),
        P("pair"),
        P("pair"),
        P("slab"),
        P("slab"),
        P(),
        P(),
    )
    return jax.shard_map(
        body, mesh=mesh, in_specs=placed, out_specs=P("pair", "slab"), check_vma=False
    )
```

```python
import functools

import jax
import jax.numpy as jnp
from jax import lax
from jax.experimental import pallas as pl
from jax.experimental.pallas import tpu as pltpu
from jax.sharding import PartitionSpec as P

MESH = pl.DeviceIdType.MESH
NT = (((1,), (1,)), ((), ()))

NZ = 8
NX = 4
ROWS = 256
KD = 384
COLS = 128
SUB = 64
PER = COLS // SUB
QUART = SUB // 2
STEPS = NZ * PER
LANES = 128
MROWS = 2 * NX * SUB
RING = 4
ORDER = (0, 1, 7, 2, 6, 3, 5, 4)
FAR = ORDER.index(4)
FIRST = (1, 2)
A_BEGIN = ((0, (3, 4)), (3, (5, 6)))
LEG1_BEGIN = 8
LEG2_BEGIN = 11
Z_BEGIN = 14
Z_END = STEPS + 2


def split(v):
    hi = v.astype(jnp.bfloat16)
    lo = (v - hi.astype(jnp.float32)).astype(jnp.bfloat16)
    return hi, lo


def ladder_kernel(
    sizes_hbm, a_hbm, b_hbm, pf_hbm, ps_hbm, af_hbm, as_hbm, occ_hbm, virt_hbm, drive_hbm, out,
    drive, drive_sem, denominator, sizes, pf, ps, af, asec, occ, virt, small_sem, a_own, a_sib, relay, b_own, b_sib, a3, b3, part, quad, done,
    r1, r2, r3, r4, mg, mh, fin,
    loc_sem, bl, bs, br, as_, ar, hs, hr, fs, fr, s1, q1, s2, q2, s3, q3, s4, q4, zs, zq, es, eq,
):
    z = lax.axis_index("pair")
    s = lax.axis_index("slab")
    x, y, c = s // (2 * NX), (s // 2) % NX, s % 2

    def slab(xx, yy, cc):
        return (xx * NX + yy) * 2 + cc

    def up(v, n, d):
        return lax.rem(v + d, n)

    xp, xo, xm = up(x, NX, 1), up(x, NX, 2), up(x, NX, 3)
    yp, yo, ym = up(y, NX, 1), up(y, NX, 2), up(y, NX, 3)
    sibling = (z, slab(x, y, 1 - c))
    side = ((z, slab(xp, y, c)), (z, slab(xm, y, c)), (z, slab(x, yp, c)), (z, slab(x, ym, c)))

    def zdev(d):
        return (up(z, NZ, d), s)

    def remote(src, dst, send, recv, dev):
        return pltpu.make_async_remote_copy(
            src_ref=src, dst_ref=dst, send_sem=send, recv_sem=recv, device_id=dev, device_id_type=MESH
        )

    barrier = pltpu.get_barrier_semaphore()
    peers = [sibling, *side] + [zdev(d) for d in range(1, NZ)]
    for dev in peers:
        pl.semaphore_signal(barrier, inc=1, device_id=dev, device_id_type=MESH)

    small = ((sizes_hbm, sizes), (pf_hbm, pf), (ps_hbm, ps), (af_hbm, af), (as_hbm, asec), (occ_hbm, occ), (virt_hbm, virt))
    small = [pltpu.make_async_copy(src, dst, small_sem.at[n]) for n, (src, dst) in enumerate(small)]

    def acols(d):
        return pl.ds(pl.multiple_of(up(z, NZ, d) * KD, KD), KD)

    def b_load(h):
        return pltpu.make_async_copy(b_hbm.at[:, c, pl.ds(h * SUB, SUB)], b_own.at[h], bl.at[h])

    def b_swap(h):
        return remote(b_hbm.at[:, 1 - c, pl.ds(h * SUB, SUB)], b_sib.at[h], bs.at[h], br.at[h], sibling)

    a_loc = pltpu.make_async_copy(a_hbm.at[:, acols(0)], a_own.at[0], loc_sem)
    a_swap = remote(a_hbm.at[:, acols(0)], a_sib.at[0], fs.at[0], fr.at[0], sibling)
    drive_copy = pltpu.make_async_copy(drive_hbm, drive, drive_sem)
    for copy in small:
        copy.start()
    b_load(0).start()
    a_loc.start()
    pl.semaphore_wait(barrier, len(peers))
    b_swap(0).start()
    a_swap.start()

    def a_send(k):
        d = NZ - ORDER[k]
        return remote(a_hbm.at[:, acols(d)], a_own.at[k], as_.at[k], ar.at[k], zdev(d))

    def leg1(h):
        rows = pl.ds(h * (ROWS // 2), ROWS // 2)
        return remote(a_hbm.at[rows, acols(4)], relay.at[h], hs.at[h], hr.at[h], zdev((2, 6)[h]))

    def leg2(h):
        rows = pl.ds(h * (ROWS // 2), ROWS // 2)
        return remote(relay.at[h], a_own.at[FAR, rows], hs.at[2 + h], hr.at[2 + h], zdev((2, 6)[h]))

    def forward(k):
        return remote(a_own.at[k], a_sib.at[k], fs.at[k], fr.at[k], sibling)

    for k in FIRST:
        a_send(k).start()
    for h in range(1, PER):
        b_swap(h).start()
        b_load(h).start()
    drive_copy.start()
    small[0].wait()

    def looked_up(table, index, width):
        entry = lax.broadcasted_iota(jnp.int32, (table.shape[1], width), 0)
        hits = jnp.where(entry == index[...], 1.0, 0.0).astype(jnp.bfloat16)
        row = jnp.broadcast_to(table[...], (8, table.shape[1]))
        hi = row.astype(jnp.bfloat16).astype(jnp.float32)
        mid = (row - hi).astype(jnp.bfloat16).astype(jnp.float32)
        term = lax.broadcasted_iota(jnp.int32, row.shape, 0)
        terms = jnp.where(term == 0, hi, jnp.where(term == 1, mid, row - hi - mid)).astype(jnp.bfloat16)
        got = lax.dot_general(terms, hits, (((1,), (0,)), ((), ())), preferred_element_type=jnp.float32)
        return got[0:1] + (got[1:2] + got[2:3])

    def energies():
        for copy in small[1:]:
            copy.wait()
        occupied = looked_up(occ, pf, ROWS) + looked_up(occ, ps, ROWS)
        rows = jnp.broadcast_to(occupied, (COLS, ROWS)).T
        first, second = looked_up(virt, af, COLS), looked_up(virt, asec, COLS)
        denominator[...] = (rows - first) - second

    energies()

    limit = sizes[s // 4]
    column = lax.broadcasted_iota(jnp.int32, (SUB, KD), 1)

    def convert(src, h, first, slab_at):
        live = column < limit - (slab_at % 4) * (NZ * KD) - z * KD

        def one(j, carry):
            hi, lo = split(jnp.where(live, src[h, j], 0.0))
            rows = pl.ds(pl.multiple_of(j * SUB, SUB), SUB)
            b3[h, rows, pl.ds(first, KD)] = hi
            b3[h, rows, pl.ds(2 * KD + first, KD)] = lo
            b3[h, rows, pl.ds(4 * KD + first, KD)] = hi
            return carry

        lax.fori_loop(0, NX * NX, one, 0)

    def send1(i):
        p = lax.rem(i, RING)
        src = (
            part.at[p, 0, xo, :, pl.ds(0, QUART)],
            part.at[p, 0, xo, :, pl.ds(QUART, QUART)],
            part.at[p, 1, :, yo, pl.ds(0, QUART)],
            part.at[p, 1, :, yo, pl.ds(QUART, QUART)],
        )
        return [remote(src[k], r1.at[p, k], s1.at[p, k], q1.at[p, k], side[k]) for k in range(4)]

    def send2(i):
        p = lax.rem(i, RING)
        src = (part.at[p, 0, xp], part.at[p, 0, xm], part.at[p, 1, :, yp], part.at[p, 1, :, ym])
        return [remote(src[k], r2.at[p, k], s2.at[p, k], q2.at[p, k], side[k]) for k in range(4)]

    def send3(i):
        p = lax.rem(i, RING)
        src = (
            quad.at[p, 1, xo, pl.ds(0, QUART)],
            quad.at[p, 1, xo, pl.ds(QUART, QUART)],
            quad.at[p, 0, yo, pl.ds(0, QUART)],
            quad.at[p, 0, yo, pl.ds(QUART, QUART)],
        )
        return [remote(src[k], r3.at[p, k], s3.at[p, k], q3.at[p, k], side[k]) for k in range(4)]

    def send4(i):
        p = lax.rem(i, RING)
        src = (quad.at[p, 1, xp], quad.at[p, 1, xm], quad.at[p, 0, yp], quad.at[p, 0, ym])
        return [remote(src[k], r4.at[p, k], s4.at[p, k], q4.at[p, k], side[k]) for k in range(4)]

    def zparts(k):
        return range(2 if k == FAR else 1)

    def zsend(k, h, part_at):
        d, i = ORDER[k], k * PER + h
        if d == 4:
            src, dst, dev = done.at[i, pl.ds(part_at * QUART, QUART)], mh.at[part_at, h], zdev(3 + 2 * part_at)
        elif d < 4:
            src, dst, dev = done.at[i], mg.at[0, d - 2, h], zdev(d - 1)
        else:
            src, dst, dev = done.at[i], mg.at[1, 6 - d, h], zdev(d + 1)
        return remote(src, dst, zs.at[k, h, part_at], zq.at[k, h, part_at], dev)

    def zstart(i):
        for k, d in enumerate(ORDER):
            if d not in (0, 1, 7):
                @pl.when(i // PER == k)
                def _():
                    for n in zparts(k):
                        zsend(k, lax.rem(i, PER), n).start()

    def last(n, h):
        i = ORDER.index((1, 7)[n]) * PER + h
        return remote(done.at[i], fin.at[n, h], es.at[n, h], eq.at[n, h], zdev((1, 7)[n]))

    def merge(n, h):
        for d in ((2, 3), (6, 5))[n]:
            zsend(ORDER.index(d), h, 0).wait_recv()
        zsend(FAR, h, n).wait_recv()
        i = ORDER.index((1, 7)[n]) * PER + h
        done[i] += mg[n, 0, h] + mg[n, 1, h]
        done[i, pl.ds(n * QUART, QUART)] += mh[n, h]
        last(n, h).start()

    def ready(n, h):
        return max(ORDER.index((1, 7)[n]), FAR) * PER + h + 5 <= Z_END

    def stage1(i):
        p = lax.rem(i, RING)
        k = i // PER
        h = lax.rem(i, PER)

        for step_at in range(PER):
            @pl.when(i == step_at)
            def _():
                b_load(step_at).wait()
                convert(b_own, step_at, 0, s)
                if step_at == 0:
                    a_loc.wait()
                b_swap(step_at).wait()
                convert(b_sib, step_at, KD, slab(x, y, 1 - c))

        @pl.when(h == 0)
        def _():
            forward(k).wait_recv()
            for first, source in ((0, a_own), (KD, a_sib)):
                hi, lo = split(source[k])
                a3[:, pl.ds(first, KD)] = hi
                a3[:, pl.ds(2 * KD + first, KD)] = hi
                a3[:, pl.ds(4 * KD + first, KD)] = lo

        def columns(m, carry):
            rows = pl.ds(pl.multiple_of(m * MROWS, MROWS), MROWS)
            acc = lax.dot_general(b3[h, rows, :], a3[...], NT, preferred_element_type=jnp.float32)
            for xx in range(2):
                for yy in range(NX):
                    at = (xx * NX + yy) * SUB
                    for half in range(2):
                        part[p, half, 2 * m + xx, yy] = acc[at:at + SUB, half * LANES:(half + 1) * LANES]
            return carry

        lax.fori_loop(0, NX // 2, columns, 0)
        for copy in send1(i):
            copy.start()

        for begin, blocks in A_BEGIN:
            @pl.when(i == begin)
            def _():
                for kk in blocks:
                    a_send(kk).start()

        @pl.when(i == LEG1_BEGIN)
        def _():
            for half in range(2):
                leg1(half).start()

    def fetch(i):
        k = i // PER

        @pl.when(k + 1 != FAR)
        def _():
            a_wait = remote(a_own.at[k + 1], a_own.at[k + 1], as_.at[k + 1], ar.at[k + 1], sibling)
            a_wait.wait_recv()

        @pl.when(k + 1 == FAR)
        def _():
            for half in range(2):
                leg2(half).wait_recv()

        forward(k + 1).start()

    def stage2(i):
        p = lax.rem(i, RING)
        for copy in send1(i):
            copy.wait()
        part[p, 0, xp, :, pl.ds(0, QUART)] += r1[p, 0]
        part[p, 0, xm, :, pl.ds(QUART, QUART)] += r1[p, 1]
        part[p, 1, :, yp, pl.ds(0, QUART)] += r1[p, 2]
        part[p, 1, :, ym, pl.ds(QUART, QUART)] += r1[p, 3]
        for copy in send2(i):
            copy.start()

    def stage3(i):
        p = lax.rem(i, RING)
        for copy in send2(i):
            copy.wait()
        quad[p, 0] = part[p, 0, x] + (r2[p, 0] + r2[p, 1])
        quad[p, 1] = part[p, 1, :, y] + (r2[p, 2] + r2[p, 3])
        for copy in send3(i):
            copy.start()

    def stage4(i):
        p = lax.rem(i, RING)
        for copy in send3(i):
            copy.wait()
        quad[p, 1, xp, pl.ds(0, QUART)] += r3[p, 0]
        quad[p, 1, xm, pl.ds(QUART, QUART)] += r3[p, 1]
        quad[p, 0, yp, pl.ds(0, QUART)] += r3[p, 2]
        quad[p, 0, ym, pl.ds(QUART, QUART)] += r3[p, 3]
        for copy in send4(i):
            copy.start()

    def stage5(i):
        p = lax.rem(i, RING)
        for copy in send4(i):
            copy.wait()
        done[i, :, pl.ds(0, LANES)] = quad[p, 0, y] + (r4[p, 2] + r4[p, 3])
        done[i, :, pl.ds(LANES, LANES)] = quad[p, 1, x] + (r4[p, 0] + r4[p, 1])

        @pl.when(i > Z_BEGIN - 4)
        def _():
            zstart(i)

    def step(i, carry):
        pl.when(jnp.logical_and(lax.rem(i, PER) == PER - 1, i < STEPS - PER))(functools.partial(fetch, i))
        for lag, stage in enumerate((stage1, stage2, stage3, stage4, stage5)):
            pl.when(jnp.logical_and(i >= lag, i < STEPS + lag))(functools.partial(stage, i - lag))

        @pl.when(i == LEG2_BEGIN)
        def _():
            for half in range(2):
                leg1(half).wait_recv()
                leg2(half).start()

        @pl.when(i == Z_BEGIN)
        def _():
            def begin(j, carry):
                zstart(j)
                return carry

            lax.fori_loop(PER, Z_BEGIN - 3, begin, 0)

        @pl.when(i == Z_END)
        def _():
            for n in range(2):
                for h in range(PER):
                    if ready(n, h):
                        merge(n, h)

        return carry

    lax.fori_loop(0, STEPS + 4, step, 0)

    for n in range(2):
        for h in range(PER):
            if not ready(n, h):
                merge(n, h)
    drive_copy.wait()
    for h in range(PER):
        for n in range(2):
            last(n, h).wait_recv()
        cols = pl.ds(h * SUB, SUB)
        ladder = (done[h] + (fin[0, h] + fin[1, h])).T
        out[:, cols] = (drive[:, cols] + ladder) / denominator[:, cols]
    for n in range(2):
        for h in range(PER):
            last(n, h).wait_send()
    for k, d in enumerate(ORDER):
        if d not in (0, 1, 7):
            for h in range(PER):
                for n in zparts(k):
                    zsend(k, h, n).wait_send()
    a_swap.wait_send()
    for k in range(1, NZ):
        forward(k).wait_send()
    for k in range(1, NZ):
        if k != FAR:
            a_send(k).wait_send()
    for half in range(2):
        leg1(half).wait_send()
        leg2(half).wait_send()


def update(amplitudes, integrals, driver, block_sizes, *tables):
    f32, bf16 = jnp.float32, jnp.bfloat16
    dma = pltpu.SemaphoreType.DMA
    scratch = [
        pltpu.VMEM((ROWS, COLS), f32), dma, pltpu.VMEM((ROWS, COLS), f32),
        pltpu.SMEM((NZ,), jnp.int32),
        *(pltpu.VMEM(table.shape, table.dtype) for table in tables),
        dma((len(tables) + 1,)),
        pltpu.VMEM((NZ, ROWS, KD), f32),
        pltpu.VMEM((NZ, ROWS, KD), f32),
        pltpu.VMEM((2, ROWS // 2, KD), f32),
        pltpu.VMEM((PER, NX * NX, SUB, KD), f32),
        pltpu.VMEM((PER, NX * NX, SUB, KD), f32),
        pltpu.VMEM((ROWS, 6 * KD), bf16),
        pltpu.VMEM((PER, NX * NX * SUB, 6 * KD), bf16),
        pltpu.VMEM((RING, 2, NX, NX, SUB, LANES), f32),
        pltpu.VMEM((RING, 2, NX, SUB, LANES), f32),
        pltpu.VMEM((STEPS, SUB, ROWS), f32),
        pltpu.VMEM((RING, 4, NX, QUART, LANES), f32),
        pltpu.VMEM((RING, 4, NX, SUB, LANES), f32),
        pltpu.VMEM((RING, 4, QUART, LANES), f32),
        pltpu.VMEM((RING, 4, SUB, LANES), f32),
        pltpu.VMEM((2, 2, PER, SUB, ROWS), f32),
        pltpu.VMEM((2, PER, QUART, ROWS), f32),
        pltpu.VMEM((2, PER, SUB, ROWS), f32),
        dma, dma((PER,)), dma((PER,)), dma((PER,)),
        dma((NZ,)), dma((NZ,)), dma((4,)), dma((4,)), dma((NZ,)), dma((NZ,)),
        dma((RING, 4)), dma((RING, 4)), dma((RING, 4)), dma((RING, 4)),
        dma((RING, 4)), dma((RING, 4)), dma((RING, 4)), dma((RING, 4)),
        dma((NZ, PER, 2)), dma((NZ, PER, 2)), dma((2, PER)), dma((2, PER)),
    ]
    return pl.pallas_call(
        ladder_kernel,
        out_shape=jax.ShapeDtypeStruct((ROWS, COLS), f32),
        in_specs=[pl.BlockSpec(memory_space=pltpu.HBM)] * (4 + len(tables)),
        out_specs=pl.BlockSpec(memory_space=pltpu.VMEM),
        scratch_shapes=scratch,
        compiler_params=pltpu.CompilerParams(
            collective_id=0, has_side_effects=True, vmem_limit_bytes=60 * 1024 * 1024
        ),
        cost_estimate=pl.CostEstimate(
            flops=3 * 2 * 2048 * 2048 * 768, bytes_accessed=12 * 1024 * 1024, transcendentals=0
        ),
        name="ladder",
    )(block_sizes, amplitudes, integrals.reshape(NX * NX, 2, COLS, KD), *tables, driver)


def body(
    amplitudes,
    integrals,
    driver,
    block_sizes,
    pair_first,
    pair_second,
    ab_first,
    ab_second,
    occ_energy,
    virt_energy,
):
    tables = (pair_first, pair_second, ab_first, ab_second, occ_energy, virt_energy)
    return update(amplitudes, integrals, driver, block_sizes, *(table[None] for table in tables))


def solution(mesh):
    placed = (
        P("pair", "slab"),
        P(None, ("slab", "pair")),
        P("pair", "slab"),
        P(),
        P("pair"),
        P("pair"),
        P("slab"),
        P("slab"),
        P(),
        P(),
    )
    return jax.shard_map(
        body, mesh=mesh, in_specs=placed, out_specs=P("pair", "slab"), check_vma=False
    )
```
